128 devices in a mesh: rep: 32 (over z, y, x_hi), tp: 4 (over x_lo, core).
Axes of the slice: x: 4 (x_hi: 2, x_lo: 2; x = x_hi * 2 + x_lo), y: 4, z: 4, core: 2. Of those that a mesh axis runs over, the one named last changes fastest.
Arguments:
- normed_input_rows: bfloat16 [4, 2048, 8192], P(None, 'rep', 'tp'), may hold values from -6 to 6
- queries: bfloat16 [4, 2048, 8192], P(None, 'rep', 'tp'), may hold values from -64 to 64
- key_weight: bfloat16 [8192, 1024], P(None, 'tp'), may hold values from -0.0625 to 0.0625
- value_weight: bfloat16 [8192, 1024], P(None, 'tp'), may hold values from -0.0625 to 0.0625
- cached_key_store: bfloat16 [2048, 256, 1024], P('rep', None, 'tp'), may hold values from -16 to 16
- cached_value_store: bfloat16 [2048, 256, 1024], P('rep', None, 'tp'), may hold values from -6 to 6
- adapter_down_weight: bfloat16 [128, 8192, 256], P('rep', 'tp'), may hold values from -0.0625 to 0.0625
- adapter_up_weight: bfloat16 [128, 2, 128, 1024], P('rep', None, None, 'tp'), may hold values from -0.5 to 0.5
- adapter_index_rows: int32 [4, 2048], P(None, 'rep'), may hold values from 0 to 127, as said below
- adapter_rank_list: int32 [128], P('rep'), may hold values from 16 to 128, as said below
- cache_fill_length: int32 [2048], P('rep'), may hold values from 2 to 256, as said below
Outputs:
- attention_out: bfloat16 [4, 2048, 8192], P(None, 'rep', 'tp')
- new_keys: bfloat16 [4, 2048, 1024], P(None, 'rep', 'tp')
- new_values: bfloat16 [4, 2048, 1024], P(None, 'rep', 'tp')
The draws below stay inside these ranges and needn't reach their ends.
Inputs may be any that keep to these rules, and one draw needn't show every extreme that they name: `adapter_index_rows`: adapter a is held on index a // 4 of rep. `adapter_rank_list`: A multiple of 16; every index of rep holds an adapter of rank 128. `cache_fill_length`: every index of rep holds a row with 256 filled slots.
All inputs are finite; a program needn't handle non-finite values.
Results may differ from the reference program's by a relative error of at most 0.0054.
Values may be sent and summed in bfloat16 or wider, within the bound.
No kernel may reach another device: no remote copies, remote signals or barrier semaphores. Data moves between devices by JAX's collectives and lax.ppermute only.
A program may use at most 128 MiB of HBM per device.

```python
import math
import jax
import jax.numpy as jnp
from jax import lax

MODEL_WIDTH = 8192
HEADS = 64
KEY_HEADS = 8
HEAD_WIDTH = 128
RANK_PADDED = 128
STEPS = 4
ROWS_DEV = 64
CTX = 256
ADP_DEV = 4
ROWS = 2048
ADAPTER_COUNT = 128
CAP = 4
N_REP = 32


def draw_queries(key, part):
    key = jax.random.fold_in(key, 7)
    normal_part = jax.random.normal(key, (STEPS, ROWS, HEADS * HEAD_WIDTH), jnp.float32)
    return jnp.clip(normal_part, -64.0, 64.0).astype(jnp.bfloat16)


def draw_cached_key_store(key, part):
    key = jax.random.fold_in(key, 5)
    normal_part = jax.random.normal(key, (ROWS, CTX, KEY_HEADS * HEAD_WIDTH), jnp.float32)
    return jnp.clip(normal_part, -16.0, 16.0).astype(jnp.bfloat16)


def draw_adapter_index_rows(key, part):
    key = jax.random.fold_in(key, 11)
    key_hot, key_first, key_order, key_shuffle, key_local = jax.random.split(key, 5)
    block_total = STEPS * N_REP
    others = (N_REP - 1) * CAP
    hottest = jax.random.randint(key_hot, (), 0, N_REP)
    leading = jax.random.randint(key_first, (STEPS, N_REP), 0, N_REP)
    leading = jnp.where(jnp.arange(STEPS)[:, None] == 0, hottest, leading).reshape(block_total)
    scores_order = jax.random.randint(key_order, (block_total, others), 0, 1 << 20) * others + jnp.arange(others)[None, :]
    ranking = jnp.argsort(scores_order, axis=-1)[:, :ROWS_DEV - CAP]
    other_homes = (leading[:, None] + 1 + ranking // CAP) % N_REP
    homes = jnp.concatenate([jnp.repeat(leading[:, None], CAP, axis=1), other_homes], axis=1)
    scores_shuffle = jax.random.randint(key_shuffle, (block_total, ROWS_DEV), 0, 1 << 20) * ROWS_DEV + jnp.arange(ROWS_DEV)[None, :]
    shuffle = jnp.argsort(scores_shuffle, axis=-1)
    homes = jnp.take_along_axis(homes, shuffle, axis=1)
    local_ids = jax.random.randint(key_local, (block_total, ROWS_DEV), 0, ADP_DEV)
    return (homes * ADP_DEV + local_ids).reshape(STEPS, ROWS).astype(jnp.int32)


def draw_adapter_rank_list(key, part):
    key = jax.random.fold_in(key, 13)
    key_ranks, key_pick = jax.random.split(key)
    ranks_drawn = 16 * jax.random.randint(key_ranks, (ADAPTER_COUNT,), 1, RANK_PADDED // 16 + 1)
    picked = jax.random.randint(key_pick, (N_REP,), 0, ADP_DEV)
    fullest = jnp.arange(ADAPTER_COUNT) % ADP_DEV == jnp.repeat(picked, ADP_DEV)
    return jnp.where(fullest, RANK_PADDED, ranks_drawn).astype(jnp.int32)


def draw_cache_fill_length(key, part):
    key = jax.random.fold_in(key, 17)
    key_raw, key_full = jax.random.split(key)
    raw_draw = jax.random.randint(key_raw, (ROWS,), 0, CTX - 1)
    length_list = 2 + raw_draw * raw_draw // CTX
    picked = jax.random.randint(key_full, (N_REP,), 0, ROWS_DEV)
    fullest = jnp.arange(ROWS) % ROWS_DEV == jnp.repeat(picked, ROWS_DEV)
    return jnp.where(fullest, CTX, length_list).astype(jnp.int32)


def block_scale(own_key, dims, pieces, least, top_value):
    loudness, own = 1.0, jax.random.fold_in(own_key, 6)
    for dim, blocks in pieces:
        draws = jnp.exp(jax.random.uniform(jax.random.fold_in(own, dim), (blocks,), jnp.float32, least / len(pieces), top_value / len(pieces)))
        loudness = loudness * jnp.repeat(draws, dims[dim] // blocks).reshape([-1 if axis == dim else 1 for axis in range(len(dims))])
    return loudness


def noise(own_key, extent, scale, reach, shards=(), held_as=jnp.bfloat16):
    values = scale * jax.random.normal(own_key, extent, jnp.float32)
    if shards:
        values = values * block_scale(own_key, extent, shards, -0.22, 0.18)
    return jnp.clip(values, -reach, reach).astype(held_as)


def setup_inputs(seed: int = 0) -> dict:
    arg_keys = jax.random.split(jax.random.key(seed), 12)
    return {
        "normed_input_rows": noise(arg_keys[0], (STEPS, ROWS, MODEL_WIDTH), 1.0, 6.0, ((1, 32), (2, 4))),
        "queries": draw_queries(jax.random.fold_in(arg_keys[11], 71), 0),
        "key_weight": noise(arg_keys[2], (MODEL_WIDTH, KEY_HEADS * HEAD_WIDTH), MODEL_WIDTH ** -0.5, 0.0625, ((1, 4),)),
        "value_weight": noise(arg_keys[3], (MODEL_WIDTH, KEY_HEADS * HEAD_WIDTH), MODEL_WIDTH ** -0.5, 0.0625, ((1, 4),)),
        "cached_key_store": draw_cached_key_store(jax.random.fold_in(arg_keys[11], 71), 0),
        "cached_value_store": noise(arg_keys[5], (ROWS, CTX, KEY_HEADS * HEAD_WIDTH), 1.0, 6.0, ((0, 32), (2, 4))),
        "adapter_down_weight": noise(arg_keys[6], (ADAPTER_COUNT, MODEL_WIDTH, 2 * RANK_PADDED), MODEL_WIDTH ** -0.5, 0.0625, ((0, 32), (1, 4))),
        "adapter_up_weight": noise(arg_keys[7], (ADAPTER_COUNT, 2, RANK_PADDED, KEY_HEADS * HEAD_WIDTH), RANK_PADDED ** -0.5, 0.5, ((0, 32), (3, 4))),
        "adapter_index_rows": draw_adapter_index_rows(jax.random.fold_in(arg_keys[11], 71), 0),
        "adapter_rank_list": draw_adapter_rank_list(jax.random.fold_in(arg_keys[11], 71), 0),
        "cache_fill_length": draw_cache_fill_length(jax.random.fold_in(arg_keys[11], 71), 0),
    }


adapter_strength = 16.0
rope_theta = 500000.0
masked_score = -1e+30

def rotate(columns, positions, head_size):
    half_size = head_size // 2
    exponent = jnp.arange(half_size, dtype=jnp.float32) * (2.0 / head_size)
    frequency = jnp.power(rope_theta, -exponent)
    angles = positions.astype(jnp.float32)[:, None] * frequency[None, :]
    cosine = jnp.cos(angles)[:, None, :]
    sine_part = jnp.sin(angles)[:, None, :]
    shaped = columns.reshape(columns.shape[0], columns.shape[1] // head_size, 2, half_size)
    lower_half = shaped[:, :, 0, :]
    upper_half = shaped[:, :, 1, :]
    turned = jnp.stack([lower_half * cosine - upper_half * sine_part, upper_half * cosine + lower_half * sine_part], axis=2)
    return turned.reshape(columns.shape)

def attend(query_rows, stored_keys, stored_values, fresh_keys, fresh_values, length_list):
    row_total = query_rows.shape[0]
    groups = stored_keys.shape[-1] // HEAD_WIDTH
    slots_total = stored_keys.shape[1]
    grouped = query_rows.astype(jnp.float32).reshape(row_total, groups, -1, HEAD_WIDTH)
    stored_key_heads = stored_keys.astype(jnp.float32).reshape(row_total, slots_total, groups, HEAD_WIDTH)
    stored_value_heads = stored_values.astype(jnp.float32).reshape(row_total, slots_total, groups, HEAD_WIDTH)
    fresh_key_heads = fresh_keys.astype(jnp.float32).reshape(fresh_keys.shape[0], row_total, groups, HEAD_WIDTH)
    fresh_value_heads = fresh_values.astype(jnp.float32).reshape(fresh_values.shape[0], row_total, groups, HEAD_WIDTH)
    score_scale = 1.0 / math.sqrt(HEAD_WIDTH)
    stored_scores = jnp.einsum('rgqd,rpgd->rgqp', grouped, stored_key_heads) * score_scale
    visible = jnp.arange(slots_total, dtype=jnp.int32)[None, None, None, :] < length_list[:, None, None, None]
    stored_scores = jnp.where(visible, stored_scores, masked_score)
    fresh_scores = jnp.einsum('rgqd,srgd->rgqs', grouped, fresh_key_heads) * score_scale
    largest = jnp.maximum(lax.optimization_barrier(jnp.max(stored_scores, axis=-1)), lax.optimization_barrier(jnp.max(fresh_scores, axis=-1)))[..., None]
    stored_weights = jnp.exp(stored_scores - largest)
    fresh_weights = jnp.exp(fresh_scores - largest)
    normalizer = lax.optimization_barrier(jnp.sum(stored_weights, axis=-1, keepdims=True)) + lax.optimization_barrier(jnp.sum(fresh_weights, axis=-1, keepdims=True))
    stored_weights = (stored_weights / normalizer).astype(jnp.bfloat16)
    fresh_weights = (fresh_weights / normalizer).astype(jnp.bfloat16)
    mixed = jnp.einsum('rgqp,rpgd->rgqd', stored_weights.astype(jnp.float32), stored_value_heads)
    mixed = mixed + jnp.einsum('rgqs,srgd->rgqd', fresh_weights.astype(jnp.float32), fresh_value_heads)
    return mixed.astype(jnp.bfloat16).reshape(row_total, -1)

def reference(normed_input_rows, queries, key_weight, value_weight, cached_key_store, cached_value_store, adapter_down_weight, adapter_up_weight, adapter_index_rows, adapter_rank_list, cache_fill_length):
    total_rows = normed_input_rows.shape[1]
    every_row = normed_input_rows.reshape(STEPS * total_rows, MODEL_WIDTH)
    every_id = adapter_index_rows.reshape(STEPS * total_rows)
    column_slot = jnp.arange(2 * RANK_PADDED, dtype=jnp.int32) % RANK_PADDED

    def adapter_term(inputs):
        single_row, adapter_slot = inputs
        inner_total = jnp.dot(single_row[None, :], adapter_down_weight[adapter_slot], preferred_element_type=jnp.float32)[0]
        selected_adapter = adapter_rank_list[adapter_slot]
        factor_matrix = jnp.where(column_slot < selected_adapter, adapter_strength / selected_adapter.astype(jnp.float32), 0.0)
        middle_state = (inner_total * factor_matrix).astype(jnp.bfloat16).reshape(2, RANK_PADDED)
        return jnp.einsum('uv,uvi->ui', middle_state.astype(jnp.float32), adapter_up_weight[adapter_slot].astype(jnp.float32))
    delta_rows = lax.map(adapter_term, (every_row, every_id)).astype(jnp.bfloat16)
    delta_rows = lax.optimization_barrier(delta_rows).astype(jnp.float32)
    base_keys = jnp.dot(every_row, key_weight, preferred_element_type=jnp.float32)
    base_values = jnp.dot(every_row, value_weight, preferred_element_type=jnp.float32)
    positions = (cache_fill_length[None, :] + jnp.arange(STEPS, dtype=jnp.int32)[:, None]).reshape(-1)
    new_keys = rotate(base_keys + delta_rows[:, 0], positions, HEAD_WIDTH).astype(jnp.bfloat16).reshape(STEPS, total_rows, KEY_HEADS * HEAD_WIDTH)
    new_values = (base_values + delta_rows[:, 1]).astype(jnp.bfloat16).reshape(STEPS, total_rows, KEY_HEADS * HEAD_WIDTH)
    blocks = total_rows // ROWS_DEV

    def split_rows(source):
        return source.reshape(STEPS, blocks, ROWS_DEV, -1).transpose(1, 0, 2, 3)

    def per_block(inputs):
        block_queries, block_keys, block_values, block_new_keys, block_new_values, block_lengths = inputs
        results = []
        for step_index in range(STEPS):
            results.append(attend(block_queries[step_index], block_keys, block_values, block_new_keys[:step_index + 1], block_new_values[:step_index + 1], block_lengths))
        return jnp.stack(results)
    attention_out = lax.map(per_block, (split_rows(queries), cached_key_store.reshape(blocks, ROWS_DEV, CTX, KEY_HEADS * HEAD_WIDTH), cached_value_store.reshape(blocks, ROWS_DEV, CTX, KEY_HEADS * HEAD_WIDTH), split_rows(new_keys), split_rows(new_values), cache_fill_length.reshape(blocks, ROWS_DEV)))
    attention_out = attention_out.transpose(1, 0, 2, 3).reshape(STEPS, total_rows, HEADS * HEAD_WIDTH)
    return (attention_out, new_keys, new_values)
```

```python
import functools
import math

import jax
import jax.numpy as jnp
from jax import lax
from jax.experimental import pallas as pl
from jax.experimental.pallas import tpu as pltpu
from jax.sharding import PartitionSpec as P

HEAD_WIDTH = 128
RANK_PADDED = 128
CAP = 4
LANES = 128

adapter_strength = 16.0
rope_theta = 500000.0
masked_score = -1e30

F32 = jnp.float32
BF16 = jnp.bfloat16
MIB = 1024 * 1024


def cost(flops, moved):
    return pl.CostEstimate(flops=int(flops), bytes_accessed=int(moved), transcendentals=0)


def params(mib, **extra):
    return pltpu.CompilerParams(vmem_limit_bytes=mib * MIB, **extra)


def dispatch_kernel(rows_dev, resident, ids_ref, x_ref, out_ref, sel_ref):
    total = x_ref.shape[0]
    width = x_ref.shape[1]
    slots = out_ref.shape[0]
    per_home = (total // rows_dev) * CAP
    ids = ids_ref[...]
    sub = lax.broadcasted_iota(jnp.int32, (total, total), 0)
    lane = lax.broadcasted_iota(jnp.int32, (total, total), 1)
    ids_r = jnp.concatenate([ids[s : s + 1] for s in range(total // rows_dev)], axis=1)
    diagonal = jnp.where(sub == lane, ids_r.astype(F32), 0.0)
    ids_c = jnp.sum(diagonal, axis=1, keepdims=True).astype(jnp.int32)
    own_r = lax.div(ids_r, resident)
    own_c = lax.div(ids_c, resident)
    same = (own_c == own_r) & (lax.div(sub, rows_dev) == lax.div(lane, rows_dev))
    before_row = jnp.sum(jnp.where(same & (sub < lane), 1.0, 0.0), axis=0, keepdims=True)
    before_col = jnp.sum(jnp.where(same & (lane < sub), 1.0, 0.0), axis=1, keepdims=True)
    step_r = lax.div(lax.broadcasted_iota(jnp.int32, (1, total), 1), rows_dev)
    step_c = lax.div(lax.broadcasted_iota(jnp.int32, (total, 1), 0), rows_dev)
    place_r = own_r * per_home + step_r * CAP + before_row.astype(jnp.int32)
    place_c = own_c * per_home + step_c * CAP + before_col.astype(jnp.int32)
    sel_ref[...] = jnp.where(
        lax.broadcasted_iota(jnp.int32, (total, slots), 1) == place_c, 1.0, 0.0
    ).astype(BF16)
    spread = jnp.where(
        lax.broadcasted_iota(jnp.int32, (slots, total), 0) == place_r, 1.0, 0.0
    ).astype(BF16)
    local = ids_c - own_c * resident
    marks = jnp.where(
        lax.broadcasted_iota(jnp.int32, (total, LANES), 1) == local, 1.0, 0.0
    ).astype(BF16)
    chunk = 512
    for start in range(0, width, chunk):
        out_ref[:, start : start + chunk] = jnp.dot(
            spread, x_ref[:, start : start + chunk], preferred_element_type=F32
        ).astype(BF16)
    out_ref[:, width:] = jnp.dot(spread, marks, preferred_element_type=F32).astype(BF16)


def dispatch(ids, x, rows_dev, resident, replicas):
    total, width = x.shape
    slots = replicas * (total // rows_dev) * CAP
    return pl.pallas_call(
        functools.partial(dispatch_kernel, rows_dev, resident),
        out_shape=(
            jax.ShapeDtypeStruct((slots, width + LANES), BF16),
            jax.ShapeDtypeStruct((total, slots), BF16),
        ),
        compiler_params=params(16),
        cost_estimate=cost(2 * slots * total * width, 2 * (total + slots) * width),
        name="dispatch",
    )(ids, x)


def mark_column(tail, index):
    lane = lax.broadcasted_iota(jnp.int32, tail.shape, 1)
    return jnp.sum(jnp.where(lane == index, tail.astype(F32), 0.0), axis=1, keepdims=True)


def down_kernel(odd_ref, landed_ref, weight_ref, factor_ref, keep_ref, send_ref, sum_ref):
    a = pl.program_id(0)
    width = weight_ref.shape[1]
    half = keep_ref.shape[0]
    product = jnp.dot(landed_ref[:, :width], weight_ref[0], preferred_element_type=F32)
    part = product * (mark_column(landed_ref[:, width:], a) * factor_ref[0])

    @pl.when(a == 0)
    def _():
        sum_ref[...] = part

    @pl.when(a > 0)
    def _():
        sum_ref[...] += part

    @pl.when(a == pl.num_programs(0) - 1)
    def _():
        odd = odd_ref[0] == 1
        low, high = sum_ref[:half], sum_ref[half:]
        keep_ref[...] = jnp.where(odd, high, low)
        send_ref[...] = jnp.where(odd, low, high)


def down(odd, landed, weight, factor):
    slots, wide = landed.shape
    count, width, ranks = weight.shape
    half = jax.ShapeDtypeStruct((slots // 2, ranks), F32)
    kept = pl.BlockSpec((slots // 2, ranks), lambda a, p: (0, 0))
    return pl.pallas_call(
        down_kernel,
        grid_spec=pltpu.PrefetchScalarGridSpec(
            num_scalar_prefetch=1,
            grid=(count,),
            in_specs=[
                pl.BlockSpec((slots, wide), lambda a, p: (0, 0)),
                pl.BlockSpec((1, width, ranks), lambda a, p: (a, 0, 0)),
                pl.BlockSpec((1, 1, ranks), lambda a, p: (a, 0, 0)),
            ],
            out_specs=(kept, kept),
            scratch_shapes=[pltpu.VMEM((slots, ranks), F32)],
        ),
        out_shape=(half, half),
        compiler_params=params(16),
        cost_estimate=cost(2 * count * slots * width * ranks, 2 * (slots * wide + count * width * ranks)),
        name="down",
    )(odd, landed, weight, factor.reshape(count, 1, ranks))


def up_kernel(odd_ref, own_ref, other_ref, tail_ref, weight_ref, out_ref):
    count, _, ranks, columns = weight_ref.shape
    odd = odd_ref[0] == 1
    tail = tail_ref[...]
    marks = [mark_column(tail, a).astype(BF16) for a in range(count)]
    own, other = own_ref[...].astype(F32), other_ref[...].astype(F32)
    whole = jnp.concatenate([jnp.where(odd, other, own), jnp.where(odd, own, other)], axis=0).astype(BF16)
    for u in range(2):
        mid = whole[:, u * ranks : (u + 1) * ranks]
        total = None
        for a in range(count):
            term = jnp.dot(mid * marks[a], weight_ref[a, u], preferred_element_type=F32)
            total = term if total is None else total + term
        out_ref[:, u * columns : (u + 1) * columns] = total.astype(BF16)


def up(odd, own, other, landed, weight):
    slots = landed.shape[0]
    count, _, ranks, columns = weight.shape
    last = landed.shape[1] // LANES - 1
    half = pl.BlockSpec(own.shape, lambda i, p: (0, 0))
    return pl.pallas_call(
        up_kernel,
        grid_spec=pltpu.PrefetchScalarGridSpec(
            num_scalar_prefetch=1,
            grid=(1,),
            in_specs=[
                half,
                half,
                pl.BlockSpec((slots, LANES), lambda i, p: (0, last)),
                pl.BlockSpec(weight.shape, lambda i, p: (0, 0, 0, 0)),
            ],
            out_specs=pl.BlockSpec((slots, 2 * columns), lambda i, p: (0, 0)),
        ),
        out_shape=jax.ShapeDtypeStruct((slots, 2 * columns), BF16),
        compiler_params=params(12),
        cost_estimate=cost(4 * count * slots * ranks * columns, 4 * slots * columns),
        name="up",
    )(odd, own, other, landed, weight)


def base_kernel(first, place_ref, *refs):
    if first:
        x0, x1, kw_ref, vw_ref, out_ref = refs
    else:
        x0, x1, kw_ref, vw_ref, before_ref, out_ref = refs
    j = pl.program_id(0)
    columns = kw_ref.shape[1]
    for index, x_ref in enumerate((x0, x1)):

        @pl.when(j == index)
        def _(index=index, x_ref=x_ref):
            for number, w_ref in enumerate((kw_ref, vw_ref)):
                term = jnp.dot(x_ref[...], w_ref[...], preferred_element_type=F32)
                where = (slice(None), slice(number * columns, (number + 1) * columns))
                if index > 0:
                    out_ref[where] += term
                elif first:
                    out_ref[where] = term
                else:
                    out_ref[where] = before_ref[where] + term


def base(places, shares, key_weight, value_weight, before=None):
    total, width = shares[0].shape
    columns = key_weight.shape[1]
    whole = pl.BlockSpec((total, width), lambda j, p: (0, 0))
    slab = pl.BlockSpec((width, columns), lambda j, p: (p[j], 0))
    result = pl.BlockSpec((total, 2 * columns), lambda j, p: (0, 0))
    more = () if before is None else (before,)
    return pl.pallas_call(
        functools.partial(base_kernel, before is None),
        grid_spec=pltpu.PrefetchScalarGridSpec(
            num_scalar_prefetch=1,
            grid=(2,),
            in_specs=[whole] * 2 + [slab] * 2 + [result] * len(more),
            out_specs=result,
        ),
        out_shape=jax.ShapeDtypeStruct((total, 2 * columns), F32),
        compiler_params=params(20),
        cost_estimate=cost(8 * total * width * columns, 4 * total * width + 8 * width * columns),
        name="base",
    )(places, *shares, key_weight, value_weight, *more)


def stored_kernel(rows, length_ref, q_ref, k_ref, v_ref, out_ref, lse_ref):
    first = pl.program_id(0) * rows
    slots = k_ref.shape[1]
    groups = k_ref.shape[2] // HEAD_WIDTH
    per_group = q_ref.shape[1] // groups
    scale = 1.0 / math.sqrt(HEAD_WIDTH)
    lane = lax.broadcasted_iota(jnp.int32, (per_group, slots), 1)
    pieces = [
        (r, slice(g * per_group, (g + 1) * per_group), slice(g * HEAD_WIDTH, (g + 1) * HEAD_WIDTH))
        for r in range(rows)
        for g in range(groups)
    ]
    raw = [
        lax.dot_general(
            q_ref[r, mine, :], k_ref[r, :, head], (((1,), (1,)), ((), ())), preferred_element_type=F32
        )
        for r, mine, head in pieces
    ]
    shares = []
    for (r, mine, head), scores in zip(pieces, raw):
        scores = jnp.where(lane < length_ref[first + r], scores * scale, masked_score)
        top = jnp.max(scores, axis=1, keepdims=True)
        weights = jnp.exp(scores - top)
        shares.append((weights.astype(BF16), top, jnp.sum(weights, axis=1, keepdims=True)))
    mixed = [
        jnp.dot(weights, v_ref[r, :, head], preferred_element_type=F32)
        for (r, mine, head), (weights, top, norm) in zip(pieces, shares)
    ]
    for (r, mine, head), (weights, top, norm), value in zip(pieces, shares, mixed):
        out_ref[r, mine, :] = value / norm
        lse_ref[r, mine, :] = jnp.broadcast_to(top + jnp.log(norm), (per_group, LANES))


def stored(lengths, q_rows, keys, values):
    count, slots, width = keys.shape
    rows = 8
    queries = q_rows.shape[1]
    block = pl.BlockSpec((rows, queries, HEAD_WIDTH), lambda i, n: (i, 0, 0))
    cache = pl.BlockSpec((rows, slots, width), lambda i, n: (i, 0, 0))
    shape = jax.ShapeDtypeStruct((count, queries, HEAD_WIDTH), F32)
    return pl.pallas_call(
        functools.partial(stored_kernel, rows),
        grid_spec=pltpu.PrefetchScalarGridSpec(
            num_scalar_prefetch=1,
            grid=(count // rows,),
            in_specs=[block, cache, cache],
            out_specs=(block, block),
        ),
        out_shape=(shape, shape),
        compiler_params=params(24),
        cost_estimate=cost(4 * count * queries * slots * HEAD_WIDTH, 4 * count * slots * width),
        name="stored",
    )(lengths, q_rows, keys, values)


def final_kernel(
    delivered_ref, sel_ref, base_ref, cos_ref, sin_ref, q_ref, old_ref, lse_ref, out_ref, key_ref, value_ref
):
    steps, block, wide = base_ref.shape
    rows = steps * block
    columns = wide // 2
    groups = columns // HEAD_WIDTH
    heads = q_ref.shape[2] // columns
    scale = 1.0 / math.sqrt(HEAD_WIDTH)
    sel = sel_ref[...].reshape(rows, sel_ref.shape[2])
    summed = base_ref[...].reshape(rows, wide) + jnp.dot(sel, delivered_ref[...], preferred_element_type=F32)
    cos = cos_ref[...].reshape(rows, HEAD_WIDTH)
    sin = sin_ref[...].reshape(rows, HEAD_WIDTH)
    ones = jnp.ones((rows, LANES), BF16)
    keys, both = [], []
    for g in range(groups):
        head = slice(g * HEAD_WIDTH, (g + 1) * HEAD_WIDTH)
        piece = summed[:, head]
        turned = (piece * cos + pltpu.roll(piece, HEAD_WIDTH // 2, 1) * sin).astype(BF16)
        keys.append(turned)
        key_ref[:, :, head] = turned.reshape(steps, block, HEAD_WIDTH)
        fresh = summed[:, columns + g * HEAD_WIDTH : columns + (g + 1) * HEAD_WIDTH].astype(BF16)
        both.append(jnp.concatenate([fresh, ones], axis=1))
        value_ref[:, :, head] = fresh.reshape(steps, block, HEAD_WIDTH)
    sub = lax.broadcasted_iota(jnp.int32, (heads * block, rows), 0)
    lane = lax.broadcasted_iota(jnp.int32, (heads * block, rows), 1)
    same_row = lax.rem(sub, block) == lax.rem(lane, block)
    of_step = lax.div(lane, block)
    pieces = [(g, t) for g in range(groups) for t in range(steps)]

    def lanes(g, h):
        return slice((g * heads + h) * HEAD_WIDTH, (g * heads + h + 1) * HEAD_WIDTH)

    raw = []
    for g, t in pieces:
        q = jnp.concatenate([q_ref[t, :, lanes(g, h)] for h in range(heads)], axis=0)
        raw.append(lax.dot_general(q, keys[g], (((1,), (1,)), ((), ())), preferred_element_type=F32))
    shares = []
    for (g, t), scores in zip(pieces, raw):
        first = (g * steps + t) * heads
        lse = lse_ref[first : first + heads].reshape(heads * block, LANES)
        scores = jnp.where(same_row & (of_step <= t), scores * scale, masked_score)
        top = jnp.maximum(lse, jnp.max(scores, axis=1, keepdims=True))
        shares.append((jnp.exp(scores - top[:, :1]).astype(BF16), jnp.exp(lse - top)))
    mixed = [jnp.dot(w, both[g], preferred_element_type=F32) for (g, t), (w, kept) in zip(pieces, shares)]
    for (g, t), (w, kept), value in zip(pieces, shares, mixed):
        first = (g * steps + t) * heads
        old = old_ref[first : first + heads].reshape(heads * block, HEAD_WIDTH)
        result = (old * kept + value[:, :HEAD_WIDTH]) / (kept + value[:, HEAD_WIDTH:])
        result = result.astype(BF16)
        for h in range(heads):
            out_ref[t, :, lanes(g, h)] = result[h * block : (h + 1) * block]


def final(delivered, sel, base_rows, cos, sin, queries, old, lse):
    steps, rows_dev, width = queries.shape
    wide = base_rows.shape[1]
    slots = sel.shape[1]
    block = min(rows_dev, LANES // steps)

    def rows_of(last):
        return pl.BlockSpec((steps, block, last), lambda i: (0, i, 0))

    def shaped(array):
        return array.reshape(steps, rows_dev, array.shape[-1])

    stored_part = pl.BlockSpec((old.shape[0], block, LANES), lambda i: (0, i, 0))
    fresh = jax.ShapeDtypeStruct((steps, rows_dev, wide // 2), BF16)
    return pl.pallas_call(
        final_kernel,
        grid=(rows_dev // block,),
        in_specs=[
            pl.BlockSpec(delivered.shape, lambda i: (0, 0)),
            rows_of(slots),
            rows_of(wide),
            rows_of(HEAD_WIDTH),
            rows_of(HEAD_WIDTH),
            rows_of(width),
            stored_part,
            stored_part,
        ],
        out_specs=(rows_of(width), rows_of(wide // 2), rows_of(wide // 2)),
        out_shape=(jax.ShapeDtypeStruct(queries.shape, BF16), fresh, fresh),
        compiler_params=params(24),
        cost_estimate=cost(1e9, 8 * MIB),
        name="final",
    )(delivered, shaped(sel), shaped(base_rows), shaped(cos), shaped(sin), queries, old, lse)


def swap(x, bit):
    count = lax.axis_size("tp")
    return lax.ppermute(x, "tp", [(i, i ^ bit) for i in range(count)])


def per_device(
    normed_input_rows,
    queries,
    key_weight,
    value_weight,
    cached_key_store,
    cached_value_store,
    adapter_down_weight,
    adapter_up_weight,
    adapter_index_rows,
    adapter_rank_list,
    cache_fill_length,
):
    steps, rows_dev, width = normed_input_rows.shape
    total = steps * rows_dev
    replicas = lax.axis_size("rep")
    resident = adapter_down_weight.shape[0]
    columns = key_weight.shape[1]
    groups = columns // HEAD_WIDTH
    heads = queries.shape[2] // columns
    t = lax.axis_index("tp")
    odd = jnp.reshape(t % 2, (1,)).astype(jnp.int32)

    x = normed_input_rows.reshape(total, width)
    outgoing, sel = dispatch(adapter_index_rows, x, rows_dev, resident, replicas)
    landed = lax.all_to_all(outgoing, "rep", split_axis=0, concat_axis=0, tiled=True)

    queries, x_near, outgoing = lax.optimization_barrier((queries, x, outgoing))
    q_rows = queries.reshape(steps, rows_dev, groups, heads, HEAD_WIDTH)
    q_rows = q_rows.transpose(1, 2, 0, 3, 4).reshape(rows_dev, groups * steps * heads, HEAD_WIDTH)
    old, lse = stored(cache_fill_length, q_rows, cached_key_store, cached_value_store)
    old = old.transpose(1, 0, 2)
    lse = lse.transpose(1, 0, 2)

    positions = (
        cache_fill_length[None, :] + jnp.arange(steps, dtype=jnp.int32)[:, None]
    ).reshape(total)
    half = HEAD_WIDTH // 2
    frequency = jnp.power(rope_theta, -(jnp.arange(half, dtype=F32) * (2.0 / HEAD_WIDTH)))
    angles = positions.astype(F32)[:, None] * frequency[None, :]
    cos, sin = jnp.cos(angles), jnp.sin(angles)
    cos = jnp.concatenate([cos, cos], axis=1)
    sin = jnp.concatenate([-sin, sin], axis=1)

    slot = jnp.arange(2 * RANK_PADDED, dtype=jnp.int32) % RANK_PADDED
    factor = jnp.where(
        slot[None, :] < adapter_rank_list[:, None],
        adapter_strength / adapter_rank_list.astype(F32)[:, None],
        0.0,
    )

    near = swap(x_near, 1)
    base_rows = base(jnp.stack([t, t ^ 1]).astype(jnp.int32), (x, near), key_weight, value_weight)
    landed, old, lse, cos, sin, base_rows, factor = lax.optimization_barrier(
        (landed, old, lse, cos, sin, base_rows, factor)
    )

    keep, send = down(odd, landed, adapter_down_weight, factor)
    part = keep + swap(send, 1)
    arrived = swap(part.astype(BF16), 2)
    x_far, arrived = lax.optimization_barrier((x, arrived))
    far = swap(x_far, 2)
    own = (part + arrived.astype(F32)).astype(BF16)
    other = swap(own, 1)
    returned = up(odd, own, other, landed, adapter_up_weight)
    delivered = lax.all_to_all(returned, "rep", split_axis=0, concat_axis=0, tiled=True)
    far, _ = lax.optimization_barrier((far, returned))
    far_near = swap(far, 1)
    base_rows = base(
        jnp.stack([t ^ 2, t ^ 3]).astype(jnp.int32), (far, far_near), key_weight, value_weight, base_rows
    )
    return final(delivered, sel, base_rows, cos, sin, queries, old, lse)


def solution(mesh):
    return jax.shard_map(
        per_device,
        mesh=mesh,
        in_specs=(
            P(None, "rep", "tp"),
            P(None, "rep", "tp"),
            P(None, "tp"),
            P(None, "tp"),
            P("rep", None, "tp"),
            P("rep", None, "tp"),
            P("rep", "tp", None),
            P("rep", None, None, "tp"),
            P(None, "rep"),
            P("rep"),
            P("rep"),
        ),
        out_specs=(P(None, "rep", "tp"), P(None, "rep", "tp"), P(None, "rep", "tp")),
        check_vma=False,
    )
```

```python
import functools
import math

import jax
import jax.numpy as jnp
from jax import lax
from jax.experimental import pallas as pl
from jax.experimental.pallas import tpu as pltpu
from jax.sharding import PartitionSpec as P

HEAD_WIDTH = 128
RANK_PADDED = 128
CAP = 4
LANES = 128

adapter_strength = 16.0
rope_theta = 500000.0
masked_score = -1e30

F32 = jnp.float32
BF16 = jnp.bfloat16
MIB = 1024 * 1024


def cost(flops, moved):
    return pl.CostEstimate(flops=int(flops), bytes_accessed=int(moved), transcendentals=0)


def params(mib, **extra):
    return pltpu.CompilerParams(vmem_limit_bytes=mib * MIB, **extra)


def dispatch_kernel(
    rows_dev, resident, ids_hbm, x_hbm, out_hbm, sel_hbm, ids_ref, x_ref, out_ref, sel_ref, in_sem, out_sem
):
    total = x_ref.shape[0]
    width = x_ref.shape[1]
    slots = out_ref.shape[0]
    per_home = (total // rows_dev) * CAP
    chunk = 512
    places = [slice(start, start + chunk) for start in range(0, width, chunk)]
    count = len(places)
    fetch_ids = pltpu.make_async_copy(ids_hbm, ids_ref, in_sem.at[count])
    fetch_ids.start()
    fetches = [
        pltpu.make_async_copy(x_hbm.at[:, where], x_ref.at[:, where], in_sem.at[i])
        for i, where in enumerate(places)
    ]
    for fetch in fetches:
        fetch.start()
    fetch_ids.wait()
    ids = ids_ref[...]
    sub = lax.broadcasted_iota(jnp.int32, (total, total), 0)
    lane = lax.broadcasted_iota(jnp.int32, (total, total), 1)
    ids_r = jnp.concatenate([ids[s : s + 1] for s in range(total // rows_dev)], axis=1)
    diagonal = jnp.where(sub == lane, ids_r.astype(F32), 0.0)
    ids_c = jnp.sum(diagonal, axis=1, keepdims=True).astype(jnp.int32)
    own_r = lax.div(ids_r, resident)
    own_c = lax.div(ids_c, resident)
    same = (own_c == own_r) & (lax.div(sub, rows_dev) == lax.div(lane, rows_dev))
    before_row = jnp.sum(jnp.where(same & (sub < lane), 1.0, 0.0), axis=0, keepdims=True)
    before_col = jnp.sum(jnp.where(same & (lane < sub), 1.0, 0.0), axis=1, keepdims=True)
    step_r = lax.div(lax.broadcasted_iota(jnp.int32, (1, total), 1), rows_dev)
    step_c = lax.div(lax.broadcasted_iota(jnp.int32, (total, 1), 0), rows_dev)
    place_r = own_r * per_home + step_r * CAP + before_row.astype(jnp.int32)
    place_c = own_c * per_home + step_c * CAP + before_col.astype(jnp.int32)
    sel_ref[...] = jnp.where(
        lax.broadcasted_iota(jnp.int32, (total, slots), 1) == place_c, 1.0, 0.0
    ).astype(BF16)
    spread = jnp.where(
        lax.broadcasted_iota(jnp.int32, (slots, total), 0) == place_r, 1.0, 0.0
    ).astype(BF16)
    local = ids_c - own_c * resident
    marks = jnp.where(
        lax.broadcasted_iota(jnp.int32, (total, LANES), 1) == local, 1.0, 0.0
    ).astype(BF16)
    sends = [pltpu.make_async_copy(sel_ref, sel_hbm, out_sem.at[count])]
    sends[0].start()
    last = slice(width, width + LANES)
    out_ref[:, last] = jnp.dot(spread, marks, preferred_element_type=F32).astype(BF16)
    sends.append(pltpu.make_async_copy(out_ref.at[:, last], out_hbm.at[:, last], out_sem.at[count + 1]))
    sends[1].start()
    for i, where in enumerate(places):
        fetches[i].wait()
        out_ref[:, where] = jnp.dot(spread, x_ref[:, where], preferred_element_type=F32).astype(BF16)
        send = pltpu.make_async_copy(out_ref.at[:, where], out_hbm.at[:, where], out_sem.at[i])
        send.start()
        sends.append(send)
    for send in sends:
        send.wait()


def in_hbm(count):
    return [pl.BlockSpec(memory_space=pltpu.HBM)] * count


def dispatch(ids, x, rows_dev, resident, replicas):
    total, width = x.shape
    slots = replicas * (total // rows_dev) * CAP
    outgoing, sel = (slots, width + LANES), (total, slots)
    return pl.pallas_call(
        functools.partial(dispatch_kernel, rows_dev, resident),
        in_specs=in_hbm(2),
        out_specs=tuple(in_hbm(2)),
        out_shape=(jax.ShapeDtypeStruct(outgoing, BF16), jax.ShapeDtypeStruct(sel, BF16)),
        scratch_shapes=[
            pltpu.VMEM(ids.shape, jnp.int32),
            pltpu.VMEM(x.shape, BF16),
            pltpu.VMEM(outgoing, BF16),
            pltpu.VMEM(sel, BF16),
            pltpu.SemaphoreType.DMA((width // 512 + 1,)),
            pltpu.SemaphoreType.DMA((width // 512 + 2,)),
        ],
        compiler_params=params(60),
        cost_estimate=cost(2 * slots * total * width, 2 * (total + slots) * width),
        name="dispatch",
    )(ids, x)


def mark_column(tail, index):
    lane = lax.broadcasted_iota(jnp.int32, tail.shape, 1)
    return jnp.sum(jnp.where(lane == index, tail.astype(F32), 0.0), axis=1, keepdims=True)


def down_kernel(odd_ref, landed_ref, weight_ref, factor_ref, keep_ref, send_ref, sum_ref):
    a = pl.program_id(0)
    width = weight_ref.shape[1]
    half = keep_ref.shape[0]
    product = jnp.dot(landed_ref[:, :width], weight_ref[0], preferred_element_type=F32)
    part = product * (mark_column(landed_ref[:, width:], a) * factor_ref[0])

    @pl.when(a == 0)
    def _():
        sum_ref[...] = part

    @pl.when(a > 0)
    def _():
        sum_ref[...] += part

    @pl.when(a == pl.num_programs(0) - 1)
    def _():
        odd = odd_ref[0] == 1
        low, high = sum_ref[:half], sum_ref[half:]
        keep_ref[...] = jnp.where(odd, high, low)
        send_ref[...] = jnp.where(odd, low, high)


def down(odd, landed, weight, factor):
    slots, wide = landed.shape
    count, width, ranks = weight.shape
    half = jax.ShapeDtypeStruct((slots // 2, ranks), F32)
    kept = pl.BlockSpec((slots // 2, ranks), lambda a, p: (0, 0))
    return pl.pallas_call(
        down_kernel,
        grid_spec=pltpu.PrefetchScalarGridSpec(
            num_scalar_prefetch=1,
            grid=(count,),
            in_specs=[
                pl.BlockSpec((slots, wide), lambda a, p: (0, 0)),
                pl.BlockSpec((1, width, ranks), lambda a, p: (a, 0, 0)),
                pl.BlockSpec((1, 1, ranks), lambda a, p: (a, 0, 0)),
            ],
            out_specs=(kept, kept),
            scratch_shapes=[pltpu.VMEM((slots, ranks), F32)],
        ),
        out_shape=(half, half),
        compiler_params=params(16),
        cost_estimate=cost(2 * count * slots * width * ranks, 2 * (slots * wide + count * width * ranks)),
        name="down",
    )(odd, landed, weight, factor.reshape(count, 1, ranks))


def up_kernel(odd_ref, own_ref, other_ref, tail_ref, weight_ref, out_ref):
    count, _, ranks, columns = weight_ref.shape
    odd = odd_ref[0] == 1
    tail = tail_ref[...]
    marks = [mark_column(tail, a).astype(BF16) for a in range(count)]
    own, other = own_ref[...].astype(F32), other_ref[...].astype(F32)
    whole = jnp.concatenate([jnp.where(odd, other, own), jnp.where(odd, own, other)], axis=0).astype(BF16)
    for u in range(2):
        mid = whole[:, u * ranks : (u + 1) * ranks]
        total = None
        for a in range(count):
            term = jnp.dot(mid * marks[a], weight_ref[a, u], preferred_element_type=F32)
            total = term if total is None else total + term
        out_ref[:, u * columns : (u + 1) * columns] = total.astype(BF16)


def up(odd, own, other, landed, weight):
    slots = landed.shape[0]
    count, _, ranks, columns = weight.shape
    last = landed.shape[1] // LANES - 1
    half = pl.BlockSpec(own.shape, lambda i, p: (0, 0))
    return pl.pallas_call(
        up_kernel,
        grid_spec=pltpu.PrefetchScalarGridSpec(
            num_scalar_prefetch=1,
            grid=(1,),
            in_specs=[
                half,
                half,
                pl.BlockSpec((slots, LANES), lambda i, p: (0, last)),
                pl.BlockSpec(weight.shape, lambda i, p: (0, 0, 0, 0)),
            ],
            out_specs=pl.BlockSpec((slots, 2 * columns), lambda i, p: (0, 0)),
        ),
        out_shape=jax.ShapeDtypeStruct((slots, 2 * columns), BF16),
        compiler_params=params(16),
        cost_estimate=cost(4 * count * slots * ranks * columns, 4 * slots * columns),
        name="up",
    )(odd, own, other, landed, weight)


def share_copies(place_ref, shares, key_hbm, value_hbm, share_refs, weight_refs, sem):
    copies = []
    for i, (share, x_ref, w_ref) in enumerate(zip(shares, share_refs, weight_refs)):
        unit = x_ref.shape[1]
        rows = pl.ds(pl.multiple_of(place_ref[i], LANES), unit)
        copies.append(
            [
                pltpu.make_async_copy(share, x_ref, sem.at[i, 0]),
                pltpu.make_async_copy(key_hbm.at[rows, :], w_ref.at[0], sem.at[i, 1]),
                pltpu.make_async_copy(value_hbm.at[rows, :], w_ref.at[1], sem.at[i, 2]),
            ]
        )
    return copies


def share_scratch(shares, columns):
    return (
        [pltpu.VMEM(x.shape, BF16) for x in shares]
        + [pltpu.VMEM((2, x.shape[1], columns), BF16) for x in shares]
        + [pltpu.SemaphoreType.DMA((max(1, len(shares)), 3))]
    )


def base_kernel(count, more, place_ref, *refs):
    shares, refs = refs[:count], refs[count:]
    key_hbm, value_hbm = refs[:2]
    before = refs[2] if more else None
    refs = refs[3:] if more else refs[2:]
    out_hbm, refs = refs[0], refs[1:]
    share_refs, weight_refs, sem = refs[:count], refs[count : 2 * count], refs[2 * count]
    out_ref, out_sem = refs[2 * count + 1 :]
    copies = share_copies(place_ref, shares, key_hbm, value_hbm, share_refs, weight_refs, sem)
    for group in copies:
        for copy in group:
            copy.start()
    if more:
        load = pltpu.make_async_copy(before, out_ref, out_sem.at[2])
        load.start()
    columns = key_hbm.shape[1]
    totals = [None, None]
    for i in range(count):
        copies[i][0].wait()
        for number in range(2):
            copies[i][1 + number].wait()
            term = jnp.dot(share_refs[i][...], weight_refs[i][number], preferred_element_type=F32)
            totals[number] = term if i == 0 else totals[number] + term
    if more:
        load.wait()
    stores = []
    for number in range(2):
        where = slice(number * columns, (number + 1) * columns)
        out_ref[:, where] = totals[number] + out_ref[:, where] if more else totals[number]
        store = pltpu.make_async_copy(out_ref.at[:, where], out_hbm.at[:, where], out_sem.at[number])
        store.start()
        stores.append(store)
    for store in stores:
        store.wait()


def base(places, shares, key_weight, value_weight, before=None):
    total = shares[0].shape[0]
    count = len(shares)
    columns = key_weight.shape[1]
    more = () if before is None else (before,)
    return pl.pallas_call(
        functools.partial(base_kernel, count, before is not None),
        in_specs=[pl.BlockSpec(memory_space=pltpu.SMEM)] + in_hbm(count + 2 + len(more)),
        out_specs=in_hbm(1)[0],
        out_shape=jax.ShapeDtypeStruct((total, 2 * columns), F32),
        scratch_shapes=share_scratch(shares, columns)
        + [pltpu.VMEM((total, 2 * columns), F32), pltpu.SemaphoreType.DMA((3,))],
        compiler_params=params(60),
        cost_estimate=cost(0, 0),
        name="base",
    )(places, *shares, key_weight, value_weight, *more)


def stored_kernel(rows, length_ref, q_ref, k_ref, v_ref, out_ref, lse_ref):
    first = pl.program_id(0) * rows
    slots = k_ref.shape[1]
    groups = k_ref.shape[2] // HEAD_WIDTH
    per_group = q_ref.shape[1] // groups
    scale = 1.0 / math.sqrt(HEAD_WIDTH)
    lane = lax.broadcasted_iota(jnp.int32, (per_group, slots), 1)
    pieces = [
        (r, slice(g * per_group, (g + 1) * per_group), slice(g * HEAD_WIDTH, (g + 1) * HEAD_WIDTH))
        for r in range(rows)
        for g in range(groups)
    ]
    raw = [
        lax.dot_general(
            q_ref[r, mine, :], k_ref[r, :, head], (((1,), (1,)), ((), ())), preferred_element_type=F32
        )
        for r, mine, head in pieces
    ]
    shares = []
    for (r, mine, head), scores in zip(pieces, raw):
        scores = jnp.where(lane < length_ref[first + r], scores * scale, masked_score)
        top = jnp.max(scores, axis=1, keepdims=True)
        weights = jnp.exp(scores - top)
        shares.append((weights.astype(BF16), top, jnp.sum(weights, axis=1, keepdims=True)))
    mixed = [
        jnp.dot(weights, v_ref[r, :, head], preferred_element_type=F32)
        for (r, mine, head), (weights, top, norm) in zip(pieces, shares)
    ]
    @pl.when(first == 0)
    def _():
        lse_ref[...] = jnp.zeros_like(lse_ref)

    logs = [[] for _ in range(rows)]
    for (r, mine, head), (weights, top, norm), value in zip(pieces, shares, mixed):
        out_ref[r, mine, :] = value / norm
        logs[r].append(top + jnp.log(norm))
    table = lse_ref[...]
    at = lax.broadcasted_iota(jnp.int32, table.shape, 1)
    for r in range(rows):
        table = jnp.where(at == first + r, jnp.concatenate(logs[r], axis=0), table)
    lse_ref[...] = table


def stored(lengths, q_rows, keys, values):
    count, slots, width = keys.shape
    rows = 8
    queries = q_rows.shape[1]
    block = pl.BlockSpec((rows, queries, HEAD_WIDTH), lambda i, n: (i, 0, 0))
    cache = pl.BlockSpec((rows, slots, width), lambda i, n: (i, 0, 0))
    return pl.pallas_call(
        functools.partial(stored_kernel, rows),
        grid_spec=pltpu.PrefetchScalarGridSpec(
            num_scalar_prefetch=1,
            grid=(count // rows,),
            in_specs=[block, cache, cache],
            out_specs=(block, pl.BlockSpec((queries, count), lambda i, n: (0, 0))),
        ),
        out_shape=(
            jax.ShapeDtypeStruct((count, queries, HEAD_WIDTH), F32),
            jax.ShapeDtypeStruct((queries, count), F32),
        ),
        compiler_params=params(60),
        cost_estimate=cost(4 * count * queries * slots * HEAD_WIDTH, 4 * count * slots * width),
        name="stored",
    )(lengths, q_rows, keys, values)


def final_kernel(steps, count, place_ref, *refs):
    shares, refs = refs[:count], refs[count:]
    key_weight, value_weight, refs = refs[0], refs[1], refs[2:]
    small, base_hbm, q_hbm, old_hbm, out_hbm, key_hbm, value_hbm = refs[:5], *refs[5:11]
    refs = refs[11:]
    share_refs, weight_refs, share_sem = refs[:count], refs[count : 2 * count], refs[2 * count]
    refs = refs[2 * count + 1 :]
    small_refs, small_sem, refs = refs[:5], refs[5], refs[6:]
    base_ref, q_ref, old_ref, out_ref, key_ref, value_ref, in_sem, out_sem, new_sem = refs
    delivered_ref, sel_ref, cos_ref, sin_ref, lse_ref = small_refs
    total, wide = base_ref.shape
    rows_dev = total // steps
    columns = wide // 2
    groups = columns // HEAD_WIDTH
    heads = q_ref.shape[2] // columns
    block = min(rows_dev, LANES // steps)
    here = steps * block
    blocks = [slice(start, start + block) for start in range(0, rows_dev, block)]
    scale = 1.0 / math.sqrt(HEAD_WIDTH)
    early = [pltpu.make_async_copy(a, b, small_sem.at[i]) for i, (a, b) in enumerate(zip(small, small_refs))]
    fetch_base = pltpu.make_async_copy(base_hbm, base_ref, in_sem.at[2 * len(blocks)])
    copies = share_copies(place_ref, shares, key_weight, value_weight, share_refs, weight_refs, share_sem)
    for copy in early[:2] + [fetch_base] + sum(copies, []) + early[2:]:
        copy.start()
    fetches = []
    for b, rows in enumerate(blocks):
        fetches.append(
            (
                pltpu.make_async_copy(q_hbm.at[:, rows, :], q_ref.at[:, rows, :], in_sem.at[2 * b]),
                pltpu.make_async_copy(old_hbm.at[:, rows, :], old_ref.at[:, rows, :], in_sem.at[2 * b + 1]),
            )
        )
        for fetch in fetches[-1]:
            fetch.start()

    for copy in early[:2]:
        copy.wait()
    delta = jnp.dot(sel_ref[...], delivered_ref[...], preferred_element_type=F32)
    fetch_base.wait()
    summed = base_ref[...] + delta
    halves = [summed[:, :columns], summed[:, columns:]]
    for i in range(count):
        copies[i][0].wait()
        for number in range(2):
            copies[i][1 + number].wait()
            halves[number] += jnp.dot(share_refs[i][...], weight_refs[i][number], preferred_element_type=F32)
    for copy in early[2:]:
        copy.wait()
    ones = jnp.ones((total, LANES), BF16)
    keys, both = [], []
    for g in range(groups):
        head = slice(g * HEAD_WIDTH, (g + 1) * HEAD_WIDTH)
        piece = halves[0][:, head]
        turned = piece * cos_ref[...] + pltpu.roll(piece, HEAD_WIDTH // 2, 1) * sin_ref[...]
        keys.append(turned.astype(BF16))
        key_ref[:, head] = keys[-1]
        fresh = halves[1][:, head].astype(BF16)
        value_ref[:, head] = fresh
        both.append(jnp.concatenate([fresh, ones], axis=1))
    sends = [
        pltpu.make_async_copy(key_ref, key_hbm, new_sem.at[0]),
        pltpu.make_async_copy(value_ref, value_hbm, new_sem.at[1]),
    ]
    for send in sends:
        send.start()

    sub = lax.broadcasted_iota(jnp.int32, (heads * block, here), 0)
    lane = lax.broadcasted_iota(jnp.int32, (heads * block, here), 1)
    same_row = lax.rem(sub, block) == lax.rem(lane, block)
    of_step = lax.div(lane, block)
    first_key = same_row & (of_step == 0)
    all_ones = jnp.ones((here, LANES), BF16)
    pieces = [(g, t) for t in range(steps) for g in range(groups)]

    def lanes(g, h):
        return slice((g * heads + h) * HEAD_WIDTH, (g * heads + h + 1) * HEAD_WIDTH)

    def of_block(array, rows):
        return jnp.concatenate(
            [array[s * rows_dev + rows.start : s * rows_dev + rows.stop] for s in range(steps)], axis=0
        )

    for b, rows in enumerate(blocks):
        own_keys = [of_block(k, rows) for k in keys]
        own_both = [of_block(v, rows) for v in both]
        logs = lse_ref[:, rows]
        logs = jnp.concatenate([logs] * steps, axis=1)
        fetches[b][0].wait()
        raw = []
        for g, t in pieces:
            q = jnp.concatenate([q_ref[t, rows, lanes(g, h)] for h in range(heads)], axis=0)
            raw.append(lax.dot_general(q, own_keys[g], (((1,), (1,)), ((), ())), preferred_element_type=F32))
        shares = []
        for (g, t), scores in zip(pieces, raw):
            first = (g * steps + t) * heads
            lse = jnp.concatenate(
                [jnp.broadcast_to(logs[first + h : first + h + 1], (block, here)) for h in range(heads)], axis=0
            )
            lse = jnp.where(first_key, lse, masked_score)
            scores = jnp.where(same_row & (of_step <= t), scores * scale, masked_score)
            top = jnp.max(jnp.maximum(lse, scores), axis=1, keepdims=True)
            shares.append((jnp.exp(scores - top).astype(BF16), jnp.exp(lse - top).astype(BF16)))
        mixed = [
            (
                jnp.dot(w, own_both[g], preferred_element_type=F32),
                jnp.dot(kept, all_ones, preferred_element_type=F32),
            )
            for (g, t), (w, kept) in zip(pieces, shares)
        ]
        fetches[b][1].wait()
        for (g, t), (value, kept) in zip(pieces, mixed):
            first = (g * steps + t) * heads
            old = old_ref[first : first + heads, rows, :].reshape(heads * block, HEAD_WIDTH)
            result = (old * kept + value[:, :HEAD_WIDTH]) / (kept + value[:, HEAD_WIDTH:])
            result = result.astype(BF16)
            for h in range(heads):
                out_ref[t, rows, lanes(g, h)] = result[h * block : (h + 1) * block]
            if g == groups - 1:
                send = pltpu.make_async_copy(
                    out_ref.at[t, rows, :], out_hbm.at[t, rows, :], out_sem.at[b * steps + t]
                )
                send.start()
                sends.append(send)
    for send in sends:
        send.wait()


def final(places, shares, key_weight, value_weight, delivered, sel, cos, sin, lse, base_rows, queries, old):
    steps, rows_dev, width = queries.shape
    total, wide = base_rows.shape
    blocks = rows_dev // min(rows_dev, LANES // steps)
    fresh = (total, wide // 2)
    count = len(shares)
    small = (delivered, sel, cos, sin, lse)
    return pl.pallas_call(
        functools.partial(final_kernel, steps, count),
        in_specs=[pl.BlockSpec(memory_space=pltpu.SMEM)] + in_hbm(count + 10),
        out_specs=tuple(in_hbm(3)),
        out_shape=(
            jax.ShapeDtypeStruct(queries.shape, BF16),
            jax.ShapeDtypeStruct(fresh, BF16),
            jax.ShapeDtypeStruct(fresh, BF16),
        ),
        scratch_shapes=share_scratch(shares, wide // 2)
        + [pltpu.VMEM(array.shape, array.dtype) for array in small]
        + [
            pltpu.SemaphoreType.DMA((len(small),)),
            pltpu.VMEM(base_rows.shape, F32),
            pltpu.VMEM(queries.shape, BF16),
            pltpu.VMEM(old.shape, F32),
            pltpu.VMEM(queries.shape, BF16),
            pltpu.VMEM(fresh, BF16),
            pltpu.VMEM(fresh, BF16),
            pltpu.SemaphoreType.DMA((2 * blocks + 1,)),
            pltpu.SemaphoreType.DMA((blocks * steps,)),
            pltpu.SemaphoreType.DMA((2,)),
        ],
        compiler_params=params(59),
        cost_estimate=cost(1e9, 8 * MIB),
        name="final",
    )(places, *shares, key_weight, value_weight, *small, base_rows, queries, old)


def swap(x, bit):
    count = lax.axis_size("tp")
    return lax.ppermute(x, "tp", [(i, i ^ bit) for i in range(count)])


def per_device(
    normed_input_rows,
    queries,
    key_weight,
    value_weight,
    cached_key_store,
    cached_value_store,
    adapter_down_weight,
    adapter_up_weight,
    adapter_index_rows,
    adapter_rank_list,
    cache_fill_length,
):
    steps, rows_dev, width = normed_input_rows.shape
    total = steps * rows_dev
    replicas = lax.axis_size("rep")
    resident = adapter_down_weight.shape[0]
    columns = key_weight.shape[1]
    groups = columns // HEAD_WIDTH
    heads = queries.shape[2] // columns
    t = lax.axis_index("tp")
    odd = jnp.reshape(t % 2, (1,)).astype(jnp.int32)

    x = normed_input_rows.reshape(total, width)
    cuts = (0, 0, 8 * width // 16, width)
    outgoing, sel = dispatch(adapter_index_rows, x, rows_dev, resident, replicas)
    landed = lax.all_to_all(outgoing, "rep", split_axis=0, concat_axis=0, tiled=True)

    queries, x_near, outgoing = lax.optimization_barrier((queries, x, outgoing))
    q_rows = queries.reshape(steps, rows_dev, groups, heads, HEAD_WIDTH)
    q_rows = q_rows.transpose(1, 2, 0, 3, 4).reshape(rows_dev, groups * steps * heads, HEAD_WIDTH)
    old, lse = stored(cache_fill_length, q_rows, cached_key_store, cached_value_store)

    positions = (
        cache_fill_length[None, :] + jnp.arange(steps, dtype=jnp.int32)[:, None]
    ).reshape(total)
    half = HEAD_WIDTH // 2
    frequency = jnp.power(rope_theta, -(jnp.arange(half, dtype=F32) * (2.0 / HEAD_WIDTH)))
    angles = positions.astype(F32)[:, None] * frequency[None, :]
    cos, sin = jnp.cos(angles), jnp.sin(angles)
    cos = jnp.concatenate([cos, cos], axis=1)
    sin = jnp.concatenate([-sin, sin], axis=1)

    slot = jnp.arange(2 * RANK_PADDED, dtype=jnp.int32) % RANK_PADDED
    factor = jnp.where(
        slot[None, :] < adapter_rank_list[:, None],
        adapter_strength / adapter_rank_list.astype(F32)[:, None],
        0.0,
    )

    near = swap(x_near, 1)
    home = jnp.stack([t, t ^ 1, t ^ 2, t ^ 3]).astype(jnp.int32) * width
    across = home[2:]
    base_rows = base(home[:2], (x, near), key_weight, value_weight)
    landed, old, lse, cos, sin, base_rows, factor = lax.optimization_barrier(
        (landed, old, lse, cos, sin, base_rows, factor)
    )

    part1, _ = lax.optimization_barrier((x_near[:, cuts[1] : cuts[2]], landed))
    far1 = swap(part1, 2)
    keep, send = down(odd, landed, adapter_down_weight, factor)
    part = keep + swap(send, 1)
    part, far1 = lax.optimization_barrier((part, far1))
    arrived = swap(part.astype(BF16), 2)
    part2, _ = lax.optimization_barrier((x_near[:, cuts[2] :], arrived))
    far2 = swap(part2, 2)
    base_rows = base(across + cuts[1], (far1, swap(far1, 1)), key_weight, value_weight, base_rows)
    own = (part + arrived.astype(F32)).astype(BF16)
    other = swap(own, 1)
    returned = up(odd, own, other, landed, adapter_up_weight)
    returned, far2, base_rows, old = lax.optimization_barrier((returned, far2, base_rows, old))
    delivered = lax.all_to_all(returned, "rep", split_axis=0, concat_axis=0, tiled=True)

    base_rows = base(across + cuts[2], (far2, swap(far2, 1)), key_weight, value_weight, base_rows)
    old = old.transpose(1, 0, 2)
    base_rows, old, delivered = lax.optimization_barrier((base_rows, old, delivered))
    out, keys, values = final(
        across, (), key_weight, value_weight,
        delivered, sel, cos, sin, lse, base_rows, queries, old,
    )
    return out, keys.reshape(steps, rows_dev, columns), values.reshape(steps, rows_dev, columns)


def solution(mesh):
    return jax.shard_map(
        per_device,
        mesh=mesh,
        in_specs=(
            P(None, "rep", "tp"),
            P(None, "rep", "tp"),
            P(None, "tp"),
            P(None, "tp"),
            P("rep", None, "tp"),
            P("rep", None, "tp"),
            P("rep", "tp", None),
            P("rep", None, None, "tp"),
            P(None, "rep"),
            P("rep"),
            P("rep"),
        ),
        out_specs=(P(None, "rep", "tp"), P(None, "rep", "tp"), P(None, "rep", "tp")),
        check_vma=False,
    )
```

```python
import functools
import math

import jax
import jax.numpy as jnp
from jax import lax
from jax.experimental import pallas as pl
from jax.experimental.pallas import tpu as pltpu
from jax.sharding import PartitionSpec as P

HEAD_WIDTH = 128
RANK_PADDED = 128
CAP = 4
LANES = 128

adapter_strength = 16.0
rope_theta = 500000.0
masked_score = -1e30

F32 = jnp.float32
BF16 = jnp.bfloat16
MIB = 1024 * 1024


def cost(flops, moved):
    return pl.CostEstimate(flops=int(flops), bytes_accessed=int(moved), transcendentals=0)


def params(mib, **extra):
    return pltpu.CompilerParams(vmem_limit_bytes=mib * MIB, **extra)


def dispatch_kernel(
    rows_dev, resident, ids_hbm, x_hbm, out_hbm, sel_hbm, ids_ref, x_ref, out_ref, sel_ref, in_sem, out_sem
):
    total = x_ref.shape[0]
    width = x_ref.shape[1]
    slots = out_ref.shape[0]
    per_home = (total // rows_dev) * CAP
    chunk = 512
    places = [slice(start, start + chunk) for start in range(0, width, chunk)]
    count = len(places)
    fetch_ids = pltpu.make_async_copy(ids_hbm, ids_ref, in_sem.at[count])
    fetch_ids.start()
    fetches = [
        pltpu.make_async_copy(x_hbm.at[:, where], x_ref.at[:, where], in_sem.at[i])
        for i, where in enumerate(places)
    ]
    for fetch in fetches:
        fetch.start()
    fetch_ids.wait()
    ids = ids_ref[...]
    sub = lax.broadcasted_iota(jnp.int32, (total, total), 0)
    lane = lax.broadcasted_iota(jnp.int32, (total, total), 1)
    ids_r = jnp.concatenate([ids[s : s + 1] for s in range(total // rows_dev)], axis=1)
    diagonal = jnp.where(sub == lane, ids_r.astype(F32), 0.0)
    ids_c = jnp.sum(diagonal, axis=1, keepdims=True).astype(jnp.int32)
    own_r = lax.div(ids_r, resident)
    own_c = lax.div(ids_c, resident)
    same = (own_c == own_r) & (lax.div(sub, rows_dev) == lax.div(lane, rows_dev))
    before_row = jnp.sum(jnp.where(same & (sub < lane), 1.0, 0.0), axis=0, keepdims=True)
    before_col = jnp.sum(jnp.where(same & (lane < sub), 1.0, 0.0), axis=1, keepdims=True)
    step_r = lax.div(lax.broadcasted_iota(jnp.int32, (1, total), 1), rows_dev)
    step_c = lax.div(lax.broadcasted_iota(jnp.int32, (total, 1), 0), rows_dev)
    place_r = own_r * per_home + step_r * CAP + before_row.astype(jnp.int32)
    place_c = own_c * per_home + step_c * CAP + before_col.astype(jnp.int32)
    sel_ref[...] = jnp.where(
        lax.broadcasted_iota(jnp.int32, (total, slots), 1) == place_c, 1.0, 0.0
    ).astype(BF16)
    spread = jnp.where(
        lax.broadcasted_iota(jnp.int32, (slots, total), 0) == place_r, 1.0, 0.0
    ).astype(BF16)
    local = ids_c - own_c * resident
    marks = jnp.where(
        lax.broadcasted_iota(jnp.int32, (total, LANES), 1) == local, 1.0, 0.0
    ).astype(BF16)
    sends = [pltpu.make_async_copy(sel_ref, sel_hbm, out_sem.at[count])]
    sends[0].start()
    last = slice(width, width + LANES)
    out_ref[:, last] = jnp.dot(spread, marks, preferred_element_type=F32).astype(BF16)
    sends.append(pltpu.make_async_copy(out_ref.at[:, last], out_hbm.at[:, last], out_sem.at[count + 1]))
    sends[1].start()
    for i, where in enumerate(places):
        fetches[i].wait()
        out_ref[:, where] = jnp.dot(spread, x_ref[:, where], preferred_element_type=F32).astype(BF16)
        send = pltpu.make_async_copy(out_ref.at[:, where], out_hbm.at[:, where], out_sem.at[i])
        send.start()
        sends.append(send)
    for send in sends:
        send.wait()


def in_hbm(count):
    return [pl.BlockSpec(memory_space=pltpu.HBM)] * count


def dispatch(ids, x, rows_dev, resident, replicas):
    total, width = x.shape
    slots = replicas * (total // rows_dev) * CAP
    outgoing, sel = (slots, width + LANES), (total, slots)
    return pl.pallas_call(
        functools.partial(dispatch_kernel, rows_dev, resident),
        in_specs=in_hbm(2),
        out_specs=tuple(in_hbm(2)),
        out_shape=(jax.ShapeDtypeStruct(outgoing, BF16), jax.ShapeDtypeStruct(sel, BF16)),
        scratch_shapes=[
            pltpu.VMEM(ids.shape, jnp.int32),
            pltpu.VMEM(x.shape, BF16),
            pltpu.VMEM(outgoing, BF16),
            pltpu.VMEM(sel, BF16),
            pltpu.SemaphoreType.DMA((width // 512 + 1,)),
            pltpu.SemaphoreType.DMA((width // 512 + 2,)),
        ],
        compiler_params=params(60),
        cost_estimate=cost(2 * slots * total * width, 2 * (total + slots) * width),
        name="dispatch",
    )(ids, x)


def mark_column(tail, index):
    lane = lax.broadcasted_iota(jnp.int32, tail.shape, 1)
    return jnp.sum(jnp.where(lane == index, tail.astype(F32), 0.0), axis=1, keepdims=True)


def down_kernel(odd_ref, landed_ref, weight_ref, factor_ref, keep_ref, send_ref, sum_ref):
    a = pl.program_id(0)
    width = weight_ref.shape[1]
    half = keep_ref.shape[0]
    product = jnp.dot(landed_ref[:, :width], weight_ref[0], preferred_element_type=F32)
    part = product * (mark_column(landed_ref[:, width:], a) * factor_ref[0])

    @pl.when(a == 0)
    def _():
        sum_ref[...] = part

    @pl.when(a > 0)
    def _():
        sum_ref[...] += part

    @pl.when(a == pl.num_programs(0) - 1)
    def _():
        odd = odd_ref[0] == 1
        low, high = sum_ref[:half], sum_ref[half:]
        keep_ref[...] = jnp.where(odd, high, low)
        send_ref[...] = jnp.where(odd, low, high)


def down(odd, landed, weight, factor):
    slots, wide = landed.shape
    count, width, ranks = weight.shape
    half = jax.ShapeDtypeStruct((slots // 2, ranks), F32)
    kept = pl.BlockSpec((slots // 2, ranks), lambda a, p: (0, 0))
    return pl.pallas_call(
        down_kernel,
        grid_spec=pltpu.PrefetchScalarGridSpec(
            num_scalar_prefetch=1,
            grid=(count,),
            in_specs=[
                pl.BlockSpec((slots, wide), lambda a, p: (0, 0)),
                pl.BlockSpec((1, width, ranks), lambda a, p: (a, 0, 0)),
                pl.BlockSpec((1, 1, ranks), lambda a, p: (a, 0, 0)),
            ],
            out_specs=(kept, kept),
            scratch_shapes=[pltpu.VMEM((slots, ranks), F32)],
        ),
        out_shape=(half, half),
        compiler_params=params(16),
        cost_estimate=cost(2 * count * slots * width * ranks, 2 * (slots * wide + count * width * ranks)),
        name="down",
    )(odd, landed, weight, factor.reshape(count, 1, ranks))


def up_kernel(odd_ref, own_ref, other_ref, tail_ref, weight_ref, out_ref):
    count, _, ranks, columns = weight_ref.shape
    odd = odd_ref[0] == 1
    tail = tail_ref[...]
    marks = [mark_column(tail, a).astype(BF16) for a in range(count)]
    own, other = own_ref[...].astype(F32), other_ref[...].astype(F32)
    whole = jnp.concatenate([jnp.where(odd, other, own), jnp.where(odd, own, other)], axis=0).astype(BF16)
    for u in range(2):
        mid = whole[:, u * ranks : (u + 1) * ranks]
        total = None
        for a in range(count):
            term = jnp.dot(mid * marks[a], weight_ref[a, u], preferred_element_type=F32)
            total = term if total is None else total + term
        out_ref[:, u * columns : (u + 1) * columns] = total.astype(BF16)


def up(odd, own, other, landed, weight):
    slots = landed.shape[0]
    count, _, ranks, columns = weight.shape
    last = landed.shape[1] // LANES - 1
    half = pl.BlockSpec(own.shape, lambda i, p: (0, 0))
    return pl.pallas_call(
        up_kernel,
        grid_spec=pltpu.PrefetchScalarGridSpec(
            num_scalar_prefetch=1,
            grid=(1,),
            in_specs=[
                half,
                half,
                pl.BlockSpec((slots, LANES), lambda i, p: (0, last)),
                pl.BlockSpec(weight.shape, lambda i, p: (0, 0, 0, 0)),
            ],
            out_specs=pl.BlockSpec((slots, 2 * columns), lambda i, p: (0, 0)),
        ),
        out_shape=jax.ShapeDtypeStruct((slots, 2 * columns), BF16),
        compiler_params=params(16),
        cost_estimate=cost(4 * count * slots * ranks * columns, 4 * slots * columns),
        name="up",
    )(odd, own, other, landed, weight)


def share_copies(place_ref, shares, key_hbm, value_hbm, share_refs, weight_refs, sem):
    copies = []
    for i, (share, x_ref, w_ref) in enumerate(zip(shares, share_refs, weight_refs)):
        unit = x_ref.shape[1]
        rows = pl.ds(pl.multiple_of(place_ref[i], LANES), unit)
        copies.append(
            [
                pltpu.make_async_copy(share, x_ref, sem.at[i, 0]),
                pltpu.make_async_copy(key_hbm.at[rows, :], w_ref.at[0], sem.at[i, 1]),
                pltpu.make_async_copy(value_hbm.at[rows, :], w_ref.at[1], sem.at[i, 2]),
            ]
        )
    return copies


def share_scratch(shares, columns):
    return (
        [pltpu.VMEM(x.shape, BF16) for x in shares]
        + [pltpu.VMEM((2, x.shape[1], columns), BF16) for x in shares]
        + [pltpu.SemaphoreType.DMA((max(1, len(shares)), 3))]
    )


def base_kernel(count, more, place_ref, *refs):
    shares, refs = refs[:count], refs[count:]
    key_hbm, value_hbm = refs[:2]
    before = refs[2] if more else None
    refs = refs[3:] if more else refs[2:]
    out_hbm, refs = refs[0], refs[1:]
    share_refs, weight_refs, sem = refs[:count], refs[count : 2 * count], refs[2 * count]
    out_ref, out_sem = refs[2 * count + 1 :]
    copies = share_copies(place_ref, shares, key_hbm, value_hbm, share_refs, weight_refs, sem)
    for group in copies:
        for copy in group:
            copy.start()
    if more:
        load = pltpu.make_async_copy(before, out_ref, out_sem.at[2])
        load.start()
    columns = key_hbm.shape[1]
    totals = [None, None]
    for i in range(count):
        copies[i][0].wait()
        for number in range(2):
            copies[i][1 + number].wait()
            term = jnp.dot(share_refs[i][...], weight_refs[i][number], preferred_element_type=F32)
            totals[number] = term if i == 0 else totals[number] + term
    if more:
        load.wait()
    stores = []
    for number in range(2):
        where = slice(number * columns, (number + 1) * columns)
        out_ref[:, where] = totals[number] + out_ref[:, where] if more else totals[number]
        store = pltpu.make_async_copy(out_ref.at[:, where], out_hbm.at[:, where], out_sem.at[number])
        store.start()
        stores.append(store)
    for store in stores:
        store.wait()


def base(places, shares, key_weight, value_weight, before=None):
    total = shares[0].shape[0]
    count = len(shares)
    columns = key_weight.shape[1]
    more = () if before is None else (before,)
    return pl.pallas_call(
        functools.partial(base_kernel, count, before is not None),
        in_specs=[pl.BlockSpec(memory_space=pltpu.SMEM)] + in_hbm(count + 2 + len(more)),
        out_specs=in_hbm(1)[0],
        out_shape=jax.ShapeDtypeStruct((total, 2 * columns), F32),
        scratch_shapes=share_scratch(shares, columns)
        + [pltpu.VMEM((total, 2 * columns), F32), pltpu.SemaphoreType.DMA((3,))],
        compiler_params=params(60),
        cost_estimate=cost(0, 0),
        name="base",
    )(places, *shares, key_weight, value_weight, *more)


def stored_kernel(rows, length_ref, q_ref, k_ref, v_ref, out_ref, lse_ref):
    first = pl.program_id(0) * rows
    slots = k_ref.shape[1]
    groups = k_ref.shape[2] // HEAD_WIDTH
    per_group = q_ref.shape[1] // groups
    scale = 1.0 / math.sqrt(HEAD_WIDTH)
    lane = lax.broadcasted_iota(jnp.int32, (per_group, slots), 1)
    pieces = [
        (r, slice(g * per_group, (g + 1) * per_group), slice(g * HEAD_WIDTH, (g + 1) * HEAD_WIDTH))
        for r in range(rows)
        for g in range(groups)
    ]
    raw = [
        lax.dot_general(
            q_ref[r, mine, :], k_ref[r, :, head], (((1,), (1,)), ((), ())), preferred_element_type=F32
        )
        for r, mine, head in pieces
    ]
    shares = []
    for (r, mine, head), scores in zip(pieces, raw):
        scores = jnp.where(lane < length_ref[first + r], scores * scale, masked_score)
        top = jnp.max(scores, axis=1, keepdims=True)
        weights = jnp.exp(scores - top)
        shares.append((weights.astype(BF16), top, jnp.sum(weights, axis=1, keepdims=True)))
    mixed = [
        jnp.dot(weights, v_ref[r, :, head], preferred_element_type=F32)
        for (r, mine, head), (weights, top, norm) in zip(pieces, shares)
    ]
    @pl.when(first == 0)
    def _():
        lse_ref[...] = jnp.zeros_like(lse_ref)

    logs = [[] for _ in range(rows)]
    for (r, mine, head), (weights, top, norm), value in zip(pieces, shares, mixed):
        out_ref[r, mine, :] = value / norm
        logs[r].append(top + jnp.log(norm))
    table = lse_ref[...]
    at = lax.broadcasted_iota(jnp.int32, table.shape, 1)
    for r in range(rows):
        table = jnp.where(at == first + r, jnp.concatenate(logs[r], axis=0), table)
    lse_ref[...] = table


def stored(lengths, q_rows, keys, values):
    count, slots, width = keys.shape
    rows = 8
    queries = q_rows.shape[1]
    block = pl.BlockSpec((rows, queries, HEAD_WIDTH), lambda i, n: (i, 0, 0))
    cache = pl.BlockSpec((rows, slots, width), lambda i, n: (i, 0, 0))
    return pl.pallas_call(
        functools.partial(stored_kernel, rows),
        grid_spec=pltpu.PrefetchScalarGridSpec(
            num_scalar_prefetch=1,
            grid=(count // rows,),
            in_specs=[block, cache, cache],
            out_specs=(block, pl.BlockSpec((queries, count), lambda i, n: (0, 0))),
        ),
        out_shape=(
            jax.ShapeDtypeStruct((count, queries, HEAD_WIDTH), F32),
            jax.ShapeDtypeStruct((queries, count), F32),
        ),
        compiler_params=params(60),
        cost_estimate=cost(4 * count * queries * slots * HEAD_WIDTH, 4 * count * slots * width),
        name="stored",
    )(lengths, q_rows, keys, values)


def final_kernel(steps, count, place_ref, *refs):
    shares, refs = refs[:count], refs[count:]
    key_weight, value_weight, refs = refs[0], refs[1], refs[2:]
    small, base_hbm, q_hbm, old_hbm, out_hbm, key_hbm, value_hbm = refs[:5], *refs[5:11]
    refs = refs[11:]
    share_refs, weight_refs, share_sem = refs[:count], refs[count : 2 * count], refs[2 * count]
    refs = refs[2 * count + 1 :]
    small_refs, small_sem, refs = refs[:5], refs[5], refs[6:]
    base_ref, q_ref, old_ref, out_ref, key_ref, value_ref, in_sem, out_sem, new_sem = refs
    delivered_ref, sel_ref, cos_ref, sin_ref, lse_ref = small_refs
    total, wide = base_ref.shape
    rows_dev = total // steps
    columns = wide // 2
    groups = columns // HEAD_WIDTH
    heads = q_ref.shape[2] // columns
    block = min(rows_dev, LANES // steps)
    here = steps * block
    blocks = [slice(start, start + block) for start in range(0, rows_dev, block)]
    scale = 1.0 / math.sqrt(HEAD_WIDTH)
    early = [pltpu.make_async_copy(a, b, small_sem.at[i]) for i, (a, b) in enumerate(zip(small, small_refs))]
    fetch_base = pltpu.make_async_copy(base_hbm, base_ref, in_sem.at[2 * len(blocks)])
    copies = share_copies(place_ref, shares, key_weight, value_weight, share_refs, weight_refs, share_sem)
    for copy in early[:2] + [fetch_base] + sum(copies, []) + early[2:]:
        copy.start()
    fetches = []
    for b, rows in enumerate(blocks):
        fetches.append(
            (
                pltpu.make_async_copy(q_hbm.at[:, rows, :], q_ref.at[:, rows, :], in_sem.at[2 * b]),
                pltpu.make_async_copy(old_hbm.at[:, rows, :], old_ref.at[:, rows, :], in_sem.at[2 * b + 1]),
            )
        )
        for fetch in fetches[-1]:
            fetch.start()

    for copy in early[:2]:
        copy.wait()
    delta = jnp.dot(sel_ref[...], delivered_ref[...], preferred_element_type=F32)
    fetch_base.wait()
    summed = base_ref[...] + delta
    halves = [summed[:, :columns], summed[:, columns:]]
    for i in range(count):
        copies[i][0].wait()
        for number in range(2):
            copies[i][1 + number].wait()
            halves[number] += jnp.dot(share_refs[i][...], weight_refs[i][number], preferred_element_type=F32)
    for copy in early[2:]:
        copy.wait()
    ones = jnp.ones((total, LANES), BF16)
    keys, both = [], []
    for g in range(groups):
        head = slice(g * HEAD_WIDTH, (g + 1) * HEAD_WIDTH)
        piece = halves[0][:, head]
        turned = piece * cos_ref[...] + pltpu.roll(piece, HEAD_WIDTH // 2, 1) * sin_ref[...]
        keys.append(turned.astype(BF16))
        key_ref[:, head] = keys[-1]
        fresh = halves[1][:, head].astype(BF16)
        value_ref[:, head] = fresh
        both.append(jnp.concatenate([fresh, ones], axis=1))
    sends = [
        pltpu.make_async_copy(key_ref, key_hbm, new_sem.at[0]),
        pltpu.make_async_copy(value_ref, value_hbm, new_sem.at[1]),
    ]
    for send in sends:
        send.start()

    sub = lax.broadcasted_iota(jnp.int32, (heads * block, here), 0)
    lane = lax.broadcasted_iota(jnp.int32, (heads * block, here), 1)
    same_row = lax.rem(sub, block) == lax.rem(lane, block)
    of_step = lax.div(lane, block)
    first_key = same_row & (of_step == 0)
    all_ones = jnp.ones((here, LANES), BF16)
    pieces = [(g, t) for t in range(steps) for g in range(groups)]

    def lanes(g, h):
        return slice((g * heads + h) * HEAD_WIDTH, (g * heads + h + 1) * HEAD_WIDTH)

    def of_block(array, rows):
        return jnp.concatenate(
            [array[s * rows_dev + rows.start : s * rows_dev + rows.stop] for s in range(steps)], axis=0
        )

    for b, rows in enumerate(blocks):
        own_keys = [of_block(k, rows) for k in keys]
        own_both = [of_block(v, rows) for v in both]
        logs = lse_ref[:, rows]
        logs = jnp.concatenate([logs] * steps, axis=1)
        fetches[b][0].wait()
        raw = []
        for g, t in pieces:
            q = jnp.concatenate([q_ref[t, rows, lanes(g, h)] for h in range(heads)], axis=0)
            raw.append(lax.dot_general(q, own_keys[g], (((1,), (1,)), ((), ())), preferred_element_type=F32))
        shares = []
        for (g, t), scores in zip(pieces, raw):
            first = (g * steps + t) * heads
            lse = jnp.concatenate(
                [jnp.broadcast_to(logs[first + h : first + h + 1], (block, here)) for h in range(heads)], axis=0
            )
            lse = jnp.where(first_key, lse, masked_score)
            scores = jnp.where(same_row & (of_step <= t), scores * scale, masked_score)
            top = jnp.max(jnp.maximum(lse, scores), axis=1, keepdims=True)
            shares.append((jnp.exp(scores - top).astype(BF16), jnp.exp(lse - top).astype(BF16)))
        mixed = [
            (
                jnp.dot(w, own_both[g], preferred_element_type=F32),
                jnp.dot(kept, all_ones, preferred_element_type=F32),
            )
            for (g, t), (w, kept) in zip(pieces, shares)
        ]
        fetches[b][1].wait()
        for (g, t), (value, kept) in zip(pieces, mixed):
            first = (g * steps + t) * heads
            old = old_ref[first : first + heads, rows, :].reshape(heads * block, HEAD_WIDTH)
            result = (old * kept + value[:, :HEAD_WIDTH]) / (kept + value[:, HEAD_WIDTH:])
            result = result.astype(BF16)
            for h in range(heads):
                out_ref[t, rows, lanes(g, h)] = result[h * block : (h + 1) * block]
            if g == groups - 1:
                send = pltpu.make_async_copy(
                    out_ref.at[t, rows, :], out_hbm.at[t, rows, :], out_sem.at[b * steps + t]
                )
                send.start()
                sends.append(send)
    for send in sends:
        send.wait()


def final(places, shares, key_weight, value_weight, delivered, sel, cos, sin, lse, base_rows, queries, old):
    steps, rows_dev, width = queries.shape
    total, wide = base_rows.shape
    blocks = rows_dev // min(rows_dev, LANES // steps)
    fresh = (total, wide // 2)
    count = len(shares)
    small = (delivered, sel, cos, sin, lse)
    return pl.pallas_call(
        functools.partial(final_kernel, steps, count),
        in_specs=[pl.BlockSpec(memory_space=pltpu.SMEM)] + in_hbm(count + 10),
        out_specs=tuple(in_hbm(3)),
        out_shape=(
            jax.ShapeDtypeStruct(queries.shape, BF16),
            jax.ShapeDtypeStruct(fresh, BF16),
            jax.ShapeDtypeStruct(fresh, BF16),
        ),
        scratch_shapes=share_scratch(shares, wide // 2)
        + [pltpu.VMEM(array.shape, array.dtype) for array in small]
        + [
            pltpu.SemaphoreType.DMA((len(small),)),
            pltpu.VMEM(base_rows.shape, F32),
            pltpu.VMEM(queries.shape, BF16),
            pltpu.VMEM(old.shape, F32),
            pltpu.VMEM(queries.shape, BF16),
            pltpu.VMEM(fresh, BF16),
            pltpu.VMEM(fresh, BF16),
            pltpu.SemaphoreType.DMA((2 * blocks + 1,)),
            pltpu.SemaphoreType.DMA((blocks * steps,)),
            pltpu.SemaphoreType.DMA((2,)),
        ],
        compiler_params=params(59),
        cost_estimate=cost(1e9, 8 * MIB),
        name="final",
    )(places, *shares, key_weight, value_weight, *small, base_rows, queries, old)


def swap(x, bit):
    count = lax.axis_size("tp")
    return lax.ppermute(x, "tp", [(i, i ^ bit) for i in range(count)])


def per_device(
    normed_input_rows,
    queries,
    key_weight,
    value_weight,
    cached_key_store,
    cached_value_store,
    adapter_down_weight,
    adapter_up_weight,
    adapter_index_rows,
    adapter_rank_list,
    cache_fill_length,
):
    steps, rows_dev, width = normed_input_rows.shape
    total = steps * rows_dev
    replicas = lax.axis_size("rep")
    resident = adapter_down_weight.shape[0]
    columns = key_weight.shape[1]
    groups = columns // HEAD_WIDTH
    heads = queries.shape[2] // columns
    t = lax.axis_index("tp")
    odd = jnp.reshape(t % 2, (1,)).astype(jnp.int32)

    x = normed_input_rows.reshape(total, width)
    cuts = (0, 7 * width // 16, 10 * width // 16, width)
    outgoing, sel = dispatch(adapter_index_rows, x, rows_dev, resident, replicas)
    landed = lax.all_to_all(outgoing, "rep", split_axis=0, concat_axis=0, tiled=True)

    queries, x_near, outgoing = lax.optimization_barrier((queries, x, outgoing))
    q_rows = queries.reshape(steps, rows_dev, groups, heads, HEAD_WIDTH)
    q_rows = q_rows.transpose(1, 2, 0, 3, 4).reshape(rows_dev, groups * steps * heads, HEAD_WIDTH)
    old, lse = stored(cache_fill_length, q_rows, cached_key_store, cached_value_store)

    positions = (
        cache_fill_length[None, :] + jnp.arange(steps, dtype=jnp.int32)[:, None]
    ).reshape(total)
    half = HEAD_WIDTH // 2
    frequency = jnp.power(rope_theta, -(jnp.arange(half, dtype=F32) * (2.0 / HEAD_WIDTH)))
    angles = positions.astype(F32)[:, None] * frequency[None, :]
    cos, sin = jnp.cos(angles), jnp.sin(angles)
    cos = jnp.concatenate([cos, cos], axis=1)
    sin = jnp.concatenate([-sin, sin], axis=1)

    slot = jnp.arange(2 * RANK_PADDED, dtype=jnp.int32) % RANK_PADDED
    factor = jnp.where(
        slot[None, :] < adapter_rank_list[:, None],
        adapter_strength / adapter_rank_list.astype(F32)[:, None],
        0.0,
    )

    near = swap(x_near, 1)
    home = jnp.stack([t, t ^ 1, t ^ 2, t ^ 3]).astype(jnp.int32) * width
    across = home[2:]
    base_rows = base(home[:2], (x, near), key_weight, value_weight)
    landed, old, lse, cos, sin, base_rows, factor = lax.optimization_barrier(
        (landed, old, lse, cos, sin, base_rows, factor)
    )

    part0, _ = lax.optimization_barrier((x_near[:, : cuts[1]], landed))
    far0 = swap(part0, 2)
    keep, send = down(odd, landed, adapter_down_weight, factor)
    part = keep + swap(send, 1)
    part, far0 = lax.optimization_barrier((part, far0))
    arrived = swap(part.astype(BF16), 2)
    part1, _ = lax.optimization_barrier((x_near[:, cuts[1] : cuts[2]], arrived))
    far1 = swap(part1, 2)
    own = (part + arrived.astype(F32)).astype(BF16)
    other = swap(own, 1)
    returned = up(odd, own, other, landed, adapter_up_weight)
    returned, far0, far1, old, part2 = lax.optimization_barrier((returned, far0, far1, old, x_near[:, cuts[2] :]))
    delivered = lax.all_to_all(returned, "rep", split_axis=0, concat_axis=0, tiled=True)

    far2 = swap(part2, 2)
    base_rows = base(
        jnp.concatenate([across, across + cuts[1]]),
        (far0, swap(far0, 1), far1, swap(far1, 1)),
        key_weight, value_weight, base_rows,
    )
    old = old.transpose(1, 0, 2)
    base_rows, old, far2 = lax.optimization_barrier((base_rows, old, far2))
    far2_near = swap(far2, 1)
    base_rows, old, far2_near, delivered = lax.optimization_barrier((base_rows, old, far2_near, delivered))
    out, keys, values = final(
        across + cuts[2], (far2, far2_near), key_weight, value_weight,
        delivered, sel, cos, sin, lse, base_rows, queries, old,
    )
    return out, keys.reshape(steps, rows_dev, columns), values.reshape(steps, rows_dev, columns)


def solution(mesh):
    return jax.shard_map(
        per_device,
        mesh=mesh,
        in_specs=(
            P(None, "rep", "tp"),
            P(None, "rep", "tp"),
            P(None, "tp"),
            P(None, "tp"),
            P("rep", None, "tp"),
            P("rep", None, "tp"),
            P("rep", "tp", None),
            P("rep", None, None, "tp"),
            P(None, "rep"),
            P("rep"),
            P("rep"),
        ),
        out_specs=(P(None, "rep", "tp"), P(None, "rep", "tp"), P(None, "rep", "tp")),
        check_vma=False,
    )
```

```python
import functools
import math

import jax
import jax.numpy as jnp
from jax import lax
from jax.experimental import pallas as pl
from jax.experimental.pallas import tpu as pltpu
from jax.sharding import PartitionSpec as P

HEAD_WIDTH = 128
RANK_PADDED = 128
CAP = 4
LANES = 128

adapter_strength = 16.0
rope_theta = 500000.0
masked_score = -1e30

F32 = jnp.float32
BF16 = jnp.bfloat16
MIB = 1024 * 1024


def cost(flops, moved):
    return pl.CostEstimate(flops=int(flops), bytes_accessed=int(moved), transcendentals=0)


def params(mib, **extra):
    return pltpu.CompilerParams(vmem_limit_bytes=mib * MIB, **extra)


def dispatch_kernel(
    rows_dev, resident, ids_hbm, x_hbm, out_hbm, sel_hbm, ids_ref, x_ref, out_ref, sel_ref, in_sem, out_sem
):
    total = x_ref.shape[0]
    width = x_ref.shape[1]
    slots = out_ref.shape[0]
    per_home = (total // rows_dev) * CAP
    chunk = 512
    places = [slice(start, start + chunk) for start in range(0, width, chunk)]
    count = len(places)
    fetch_ids = pltpu.make_async_copy(ids_hbm, ids_ref, in_sem.at[count])
    fetch_ids.start()
    fetches = [
        pltpu.make_async_copy(x_hbm.at[:, where], x_ref.at[:, where], in_sem.at[i])
        for i, where in enumerate(places)
    ]
    for fetch in fetches:
        fetch.start()
    fetch_ids.wait()
    ids = ids_ref[...]
    sub = lax.broadcasted_iota(jnp.int32, (total, total), 0)
    lane = lax.broadcasted_iota(jnp.int32, (total, total), 1)
    ids_r = jnp.concatenate([ids[s : s + 1] for s in range(total // rows_dev)], axis=1)
    diagonal = jnp.where(sub == lane, ids_r.astype(F32), 0.0)
    ids_c = jnp.sum(diagonal, axis=1, keepdims=True).astype(jnp.int32)
    own_r = lax.div(ids_r, resident)
    own_c = lax.div(ids_c, resident)
    same = (own_c == own_r) & (lax.div(sub, rows_dev) == lax.div(lane, rows_dev))
    before_row = jnp.sum(jnp.where(same & (sub < lane), 1.0, 0.0), axis=0, keepdims=True)
    before_col = jnp.sum(jnp.where(same & (lane < sub), 1.0, 0.0), axis=1, keepdims=True)
    step_r = lax.div(lax.broadcasted_iota(jnp.int32, (1, total), 1), rows_dev)
    step_c = lax.div(lax.broadcasted_iota(jnp.int32, (total, 1), 0), rows_dev)
    place_r = own_r * per_home + step_r * CAP + before_row.astype(jnp.int32)
    place_c = own_c * per_home + step_c * CAP + before_col.astype(jnp.int32)
    sel_ref[...] = jnp.where(
        lax.broadcasted_iota(jnp.int32, (total, slots), 1) == place_c, 1.0, 0.0
    ).astype(BF16)
    spread = jnp.where(
        lax.broadcasted_iota(jnp.int32, (slots, total), 0) == place_r, 1.0, 0.0
    ).astype(BF16)
    local = ids_c - own_c * resident
    marks = jnp.where(
        lax.broadcasted_iota(jnp.int32, (total, LANES), 1) == local, 1.0, 0.0
    ).astype(BF16)
    sends = [pltpu.make_async_copy(sel_ref, sel_hbm, out_sem.at[count])]
    sends[0].start()
    last = slice(width, width + LANES)
    out_ref[:, last] = jnp.dot(spread, marks, preferred_element_type=F32).astype(BF16)
    sends.append(pltpu.make_async_copy(out_ref.at[:, last], out_hbm.at[:, last], out_sem.at[count + 1]))
    sends[1].start()
    for i, where in enumerate(places):
        fetches[i].wait()
        out_ref[:, where] = jnp.dot(spread, x_ref[:, where], preferred_element_type=F32).astype(BF16)
        send = pltpu.make_async_copy(out_ref.at[:, where], out_hbm.at[:, where], out_sem.at[i])
        send.start()
        sends.append(send)
    for send in sends:
        send.wait()


def in_hbm(count):
    return [pl.BlockSpec(memory_space=pltpu.HBM)] * count


def dispatch(ids, x, rows_dev, resident, replicas):
    total, width = x.shape
    slots = replicas * (total // rows_dev) * CAP
    outgoing, sel = (slots, width + LANES), (total, slots)
    return pl.pallas_call(
        functools.partial(dispatch_kernel, rows_dev, resident),
        in_specs=in_hbm(2),
        out_specs=tuple(in_hbm(2)),
        out_shape=(jax.ShapeDtypeStruct(outgoing, BF16), jax.ShapeDtypeStruct(sel, BF16)),
        scratch_shapes=[
            pltpu.VMEM(ids.shape, jnp.int32),
            pltpu.VMEM(x.shape, BF16),
            pltpu.VMEM(outgoing, BF16),
            pltpu.VMEM(sel, BF16),
            pltpu.SemaphoreType.DMA((width // 512 + 1,)),
            pltpu.SemaphoreType.DMA((width // 512 + 2,)),
        ],
        compiler_params=params(60),
        cost_estimate=cost(2 * slots * total * width, 2 * (total + slots) * width),
        name="dispatch",
    )(ids, x)


def mark_column(tail, index):
    lane = lax.broadcasted_iota(jnp.int32, tail.shape, 1)
    return jnp.sum(jnp.where(lane == index, tail.astype(F32), 0.0), axis=1, keepdims=True)


def down_kernel(odd_ref, landed_ref, weight_ref, factor_ref, keep_ref, send_ref, sum_ref):
    a = pl.program_id(0)
    width = weight_ref.shape[1]
    half = keep_ref.shape[0]
    product = jnp.dot(landed_ref[:, :width], weight_ref[0], preferred_element_type=F32)
    part = product * (mark_column(landed_ref[:, width:], a) * factor_ref[0])

    @pl.when(a == 0)
    def _():
        sum_ref[...] = part

    @pl.when(a > 0)
    def _():
        sum_ref[...] += part

    @pl.when(a == pl.num_programs(0) - 1)
    def _():
        odd = odd_ref[0] == 1
        low, high = sum_ref[:half], sum_ref[half:]
        keep_ref[...] = jnp.where(odd, high, low)
        send_ref[...] = jnp.where(odd, low, high)


def down(odd, landed, weight, factor):
    slots, wide = landed.shape
    count, width, ranks = weight.shape
    half = jax.ShapeDtypeStruct((slots // 2, ranks), F32)
    kept = pl.BlockSpec((slots // 2, ranks), lambda a, p: (0, 0))
    return pl.pallas_call(
        down_kernel,
        grid_spec=pltpu.PrefetchScalarGridSpec(
            num_scalar_prefetch=1,
            grid=(count,),
            in_specs=[
                pl.BlockSpec((slots, wide), lambda a, p: (0, 0)),
                pl.BlockSpec((1, width, ranks), lambda a, p: (a, 0, 0)),
                pl.BlockSpec((1, 1, ranks), lambda a, p: (a, 0, 0)),
            ],
            out_specs=(kept, kept),
            scratch_shapes=[pltpu.VMEM((slots, ranks), F32)],
        ),
        out_shape=(half, half),
        compiler_params=params(16),
        cost_estimate=cost(2 * count * slots * width * ranks, 2 * (slots * wide + count * width * ranks)),
        name="down",
    )(odd, landed, weight, factor.reshape(count, 1, ranks))


def up_kernel(odd_ref, own_ref, other_ref, tail_ref, weight_ref, out_ref):
    count, _, ranks, columns = weight_ref.shape
    odd = odd_ref[0] == 1
    tail = tail_ref[...]
    marks = [mark_column(tail, a).astype(BF16) for a in range(count)]
    own, other = own_ref[...].astype(F32), other_ref[...].astype(F32)
    whole = jnp.concatenate([jnp.where(odd, other, own), jnp.where(odd, own, other)], axis=0).astype(BF16)
    for u in range(2):
        mid = whole[:, u * ranks : (u + 1) * ranks]
        total = None
        for a in range(count):
            term = jnp.dot(mid * marks[a], weight_ref[a, u], preferred_element_type=F32)
            total = term if total is None else total + term
        out_ref[:, u * columns : (u + 1) * columns] = total.astype(BF16)


def up(odd, own, other, landed, weight):
    slots = landed.shape[0]
    count, _, ranks, columns = weight.shape
    last = landed.shape[1] // LANES - 1
    half = pl.BlockSpec(own.shape, lambda i, p: (0, 0))
    return pl.pallas_call(
        up_kernel,
        grid_spec=pltpu.PrefetchScalarGridSpec(
            num_scalar_prefetch=1,
            grid=(1,),
            in_specs=[
                half,
                half,
                pl.BlockSpec((slots, LANES), lambda i, p: (0, last)),
                pl.BlockSpec(weight.shape, lambda i, p: (0, 0, 0, 0)),
            ],
            out_specs=pl.BlockSpec((slots, 2 * columns), lambda i, p: (0, 0)),
        ),
        out_shape=jax.ShapeDtypeStruct((slots, 2 * columns), BF16),
        compiler_params=params(16),
        cost_estimate=cost(4 * count * slots * ranks * columns, 4 * slots * columns),
        name="up",
    )(odd, own, other, landed, weight)


def share_copies(place_ref, shares, key_hbm, value_hbm, share_refs, weight_refs, sem):
    copies = []
    for i, (share, x_ref, w_ref) in enumerate(zip(shares, share_refs, weight_refs)):
        unit = x_ref.shape[1]
        rows = pl.ds(pl.multiple_of(place_ref[i], LANES), unit)
        copies.append(
            [
                pltpu.make_async_copy(share, x_ref, sem.at[i, 0]),
                pltpu.make_async_copy(key_hbm.at[rows, :], w_ref.at[0], sem.at[i, 1]),
                pltpu.make_async_copy(value_hbm.at[rows, :], w_ref.at[1], sem.at[i, 2]),
            ]
        )
    return copies


def share_scratch(shares, columns):
    return (
        [pltpu.VMEM(x.shape, BF16) for x in shares]
        + [pltpu.VMEM((2, x.shape[1], columns), BF16) for x in shares]
        + [pltpu.SemaphoreType.DMA((max(1, len(shares)), 3))]
    )


def base_kernel(count, more, place_ref, *refs):
    shares, refs = refs[:count], refs[count:]
    key_hbm, value_hbm = refs[:2]
    before = refs[2] if more else None
    refs = refs[3:] if more else refs[2:]
    out_hbm, refs = refs[0], refs[1:]
    share_refs, weight_refs, sem = refs[:count], refs[count : 2 * count], refs[2 * count]
    out_ref, out_sem = refs[2 * count + 1 :]
    copies = share_copies(place_ref, shares, key_hbm, value_hbm, share_refs, weight_refs, sem)
    for group in copies:
        for copy in group:
            copy.start()
    if more:
        load = pltpu.make_async_copy(before, out_ref, out_sem.at[2])
        load.start()
    columns = key_hbm.shape[1]
    totals = [None, None]
    for i in range(count):
        copies[i][0].wait()
        for number in range(2):
            copies[i][1 + number].wait()
            term = jnp.dot(share_refs[i][...], weight_refs[i][number], preferred_element_type=F32)
            totals[number] = term if i == 0 else totals[number] + term
    if more:
        load.wait()
    stores = []
    for number in range(2):
        where = slice(number * columns, (number + 1) * columns)
        out_ref[:, where] = totals[number] + out_ref[:, where] if more else totals[number]
        store = pltpu.make_async_copy(out_ref.at[:, where], out_hbm.at[:, where], out_sem.at[number])
        store.start()
        stores.append(store)
    for store in stores:
        store.wait()


def base(places, shares, key_weight, value_weight, before=None):
    total = shares[0].shape[0]
    count = len(shares)
    columns = key_weight.shape[1]
    more = () if before is None else (before,)
    return pl.pallas_call(
        functools.partial(base_kernel, count, before is not None),
        in_specs=[pl.BlockSpec(memory_space=pltpu.SMEM)] + in_hbm(count + 2 + len(more)),
        out_specs=in_hbm(1)[0],
        out_shape=jax.ShapeDtypeStruct((total, 2 * columns), F32),
        scratch_shapes=share_scratch(shares, columns)
        + [pltpu.VMEM((total, 2 * columns), F32), pltpu.SemaphoreType.DMA((3,))],
        compiler_params=params(60),
        cost_estimate=cost(0, 0),
        name="base",
    )(places, *shares, key_weight, value_weight, *more)


def stored_kernel(rows, length_ref, q_ref, k_ref, v_ref, out_ref, lse_ref):
    first = pl.program_id(0) * rows
    slots = k_ref.shape[1]
    groups = k_ref.shape[2] // HEAD_WIDTH
    per_group = q_ref.shape[1] // groups
    scale = 1.0 / math.sqrt(HEAD_WIDTH)
    lane = lax.broadcasted_iota(jnp.int32, (per_group, slots), 1)
    pieces = [
        (r, slice(g * per_group, (g + 1) * per_group), slice(g * HEAD_WIDTH, (g + 1) * HEAD_WIDTH))
        for r in range(rows)
        for g in range(groups)
    ]
    raw = [
        lax.dot_general(
            q_ref[r, mine, :], k_ref[r, :, head], (((1,), (1,)), ((), ())), preferred_element_type=F32
        )
        for r, mine, head in pieces
    ]
    shares = []
    for (r, mine, head), scores in zip(pieces, raw):
        scores = jnp.where(lane < length_ref[first + r], scores * scale, masked_score)
        top = jnp.max(scores, axis=1, keepdims=True)
        weights = jnp.exp(scores - top)
        shares.append((weights.astype(BF16), top, jnp.sum(weights, axis=1, keepdims=True)))
    mixed = [
        jnp.dot(weights, v_ref[r, :, head], preferred_element_type=F32)
        for (r, mine, head), (weights, top, norm) in zip(pieces, shares)
    ]
    @pl.when(first == 0)
    def _():
        lse_ref[...] = jnp.zeros_like(lse_ref)

    logs = [[] for _ in range(rows)]
    for (r, mine, head), (weights, top, norm), value in zip(pieces, shares, mixed):
        out_ref[r, mine, :] = value / norm
        logs[r].append(top + jnp.log(norm))
    table = lse_ref[...]
    at = lax.broadcasted_iota(jnp.int32, table.shape, 1)
    for r in range(rows):
        table = jnp.where(at == first + r, jnp.concatenate(logs[r], axis=0), table)
    lse_ref[...] = table


def stored(lengths, q_rows, keys, values):
    count, slots, width = keys.shape
    rows = 8
    queries = q_rows.shape[1]
    block = pl.BlockSpec((rows, queries, HEAD_WIDTH), lambda i, n: (i, 0, 0))
    cache = pl.BlockSpec((rows, slots, width), lambda i, n: (i, 0, 0))
    return pl.pallas_call(
        functools.partial(stored_kernel, rows),
        grid_spec=pltpu.PrefetchScalarGridSpec(
            num_scalar_prefetch=1,
            grid=(count // rows,),
            in_specs=[block, cache, cache],
            out_specs=(block, pl.BlockSpec((queries, count), lambda i, n: (0, 0))),
        ),
        out_shape=(
            jax.ShapeDtypeStruct((count, queries, HEAD_WIDTH), F32),
            jax.ShapeDtypeStruct((queries, count), F32),
        ),
        compiler_params=params(60),
        cost_estimate=cost(4 * count * queries * slots * HEAD_WIDTH, 4 * count * slots * width),
        name="stored",
    )(lengths, q_rows, keys, values)


def final_kernel(steps, count, place_ref, *refs):
    shares, refs = refs[:count], refs[count:]
    key_weight, value_weight, refs = refs[0], refs[1], refs[2:]
    small, base_hbm, q_hbm, old_hbm, out_hbm, key_hbm, value_hbm = refs[:5], *refs[5:11]
    refs = refs[11:]
    share_refs, weight_refs, share_sem = refs[:count], refs[count : 2 * count], refs[2 * count]
    refs = refs[2 * count + 1 :]
    small_refs, small_sem, refs = refs[:5], refs[5], refs[6:]
    base_ref, q_ref, old_ref, out_ref, key_ref, value_ref, in_sem, out_sem, new_sem = refs
    delivered_ref, sel_ref, cos_ref, sin_ref, lse_ref = small_refs
    total, wide = base_ref.shape
    rows_dev = total // steps
    columns = wide // 2
    groups = columns // HEAD_WIDTH
    heads = q_ref.shape[2] // columns
    block = min(rows_dev, LANES // steps)
    here = steps * block
    blocks = [slice(start, start + block) for start in range(0, rows_dev, block)]
    scale = 1.0 / math.sqrt(HEAD_WIDTH)
    early = [pltpu.make_async_copy(a, b, small_sem.at[i]) for i, (a, b) in enumerate(zip(small, small_refs))]
    fetch_base = pltpu.make_async_copy(base_hbm, base_ref, in_sem.at[2 * len(blocks)])
    copies = share_copies(place_ref, shares, key_weight, value_weight, share_refs, weight_refs, share_sem)
    for copy in early[:2] + [fetch_base] + sum(copies, []) + early[2:]:
        copy.start()
    fetches = []
    for b, rows in enumerate(blocks):
        fetches.append(
            (
                pltpu.make_async_copy(q_hbm.at[:, rows, :], q_ref.at[:, rows, :], in_sem.at[2 * b]),
                pltpu.make_async_copy(old_hbm.at[:, rows, :], old_ref.at[:, rows, :], in_sem.at[2 * b + 1]),
            )
        )
        for fetch in fetches[-1]:
            fetch.start()

    for copy in early[:2]:
        copy.wait()
    delta = jnp.dot(sel_ref[...], delivered_ref[...], preferred_element_type=F32)
    fetch_base.wait()
    summed = base_ref[...] + delta
    halves = [summed[:, :columns], summed[:, columns:]]
    for i in range(count):
        copies[i][0].wait()
        for number in range(2):
            copies[i][1 + number].wait()
            halves[number] += jnp.dot(share_refs[i][...], weight_refs[i][number], preferred_element_type=F32)
    for copy in early[2:]:
        copy.wait()
    ones = jnp.ones((total, LANES), BF16)
    keys, both = [], []
    for g in range(groups):
        head = slice(g * HEAD_WIDTH, (g + 1) * HEAD_WIDTH)
        piece = halves[0][:, head]
        turned = piece * cos_ref[...] + pltpu.roll(piece, HEAD_WIDTH // 2, 1) * sin_ref[...]
        keys.append(turned.astype(BF16))
        key_ref[:, head] = keys[-1]
        fresh = halves[1][:, head].astype(BF16)
        value_ref[:, head] = fresh
        both.append(jnp.concatenate([fresh, ones], axis=1))
    sends = [
        pltpu.make_async_copy(key_ref, key_hbm, new_sem.at[0]),
        pltpu.make_async_copy(value_ref, value_hbm, new_sem.at[1]),
    ]
    for send in sends:
        send.start()

    sub = lax.broadcasted_iota(jnp.int32, (heads * block, here), 0)
    lane = lax.broadcasted_iota(jnp.int32, (heads * block, here), 1)
    same_row = lax.rem(sub, block) == lax.rem(lane, block)
    of_step = lax.div(lane, block)
    first_key = same_row & (of_step == 0)
    all_ones = jnp.ones((here, LANES), BF16)
    pieces = [(g, t) for t in range(steps) for g in range(groups)]

    def lanes(g, h):
        return slice((g * heads + h) * HEAD_WIDTH, (g * heads + h + 1) * HEAD_WIDTH)

    def of_block(array, rows):
        return jnp.concatenate(
            [array[s * rows_dev + rows.start : s * rows_dev + rows.stop] for s in range(steps)], axis=0
        )

    for b, rows in enumerate(blocks):
        own_keys = [of_block(k, rows) for k in keys]
        own_both = [of_block(v, rows) for v in both]
        logs = lse_ref[:, rows]
        logs = jnp.concatenate([logs] * steps, axis=1)
        fetches[b][0].wait()
        raw = []
        for g, t in pieces:
            q = jnp.concatenate([q_ref[t, rows, lanes(g, h)] for h in range(heads)], axis=0)
            raw.append(lax.dot_general(q, own_keys[g], (((1,), (1,)), ((), ())), preferred_element_type=F32))
        shares = []
        for (g, t), scores in zip(pieces, raw):
            first = (g * steps + t) * heads
            lse = jnp.concatenate(
                [jnp.broadcast_to(logs[first + h : first + h + 1], (block, here)) for h in range(heads)], axis=0
            )
            lse = jnp.where(first_key, lse, masked_score)
            scores = jnp.where(same_row & (of_step <= t), scores * scale, masked_score)
            top = jnp.max(jnp.maximum(lse, scores), axis=1, keepdims=True)
            shares.append((jnp.exp(scores - top).astype(BF16), jnp.exp(lse - top).astype(BF16)))
        mixed = [
            (
                jnp.dot(w, own_both[g], preferred_element_type=F32),
                jnp.dot(kept, all_ones, preferred_element_type=F32),
            )
            for (g, t), (w, kept) in zip(pieces, shares)
        ]
        fetches[b][1].wait()
        for (g, t), (value, kept) in zip(pieces, mixed):
            first = (g * steps + t) * heads
            old = old_ref[first : first + heads, rows, :].reshape(heads * block, HEAD_WIDTH)
            result = (old * kept + value[:, :HEAD_WIDTH]) / (kept + value[:, HEAD_WIDTH:])
            result = result.astype(BF16)
            for h in range(heads):
                out_ref[t, rows, lanes(g, h)] = result[h * block : (h + 1) * block]
            if g == groups - 1:
                send = pltpu.make_async_copy(
                    out_ref.at[t, rows, :], out_hbm.at[t, rows, :], out_sem.at[b * steps + t]
                )
                send.start()
                sends.append(send)
    for send in sends:
        send.wait()


def final(places, shares, key_weight, value_weight, delivered, sel, cos, sin, lse, base_rows, queries, old):
    steps, rows_dev, width = queries.shape
    total, wide = base_rows.shape
    blocks = rows_dev // min(rows_dev, LANES // steps)
    fresh = (total, wide // 2)
    count = len(shares)
    small = (delivered, sel, cos, sin, lse)
    return pl.pallas_call(
        functools.partial(final_kernel, steps, count),
        in_specs=[pl.BlockSpec(memory_space=pltpu.SMEM)] + in_hbm(count + 10),
        out_specs=tuple(in_hbm(3)),
        out_shape=(
            jax.ShapeDtypeStruct(queries.shape, BF16),
            jax.ShapeDtypeStruct(fresh, BF16),
            jax.ShapeDtypeStruct(fresh, BF16),
        ),
        scratch_shapes=share_scratch(shares, wide // 2)
        + [pltpu.VMEM(array.shape, array.dtype) for array in small]
        + [
            pltpu.SemaphoreType.DMA((len(small),)),
            pltpu.VMEM(base_rows.shape, F32),
            pltpu.VMEM(queries.shape, BF16),
            pltpu.VMEM(old.shape, F32),
            pltpu.VMEM(queries.shape, BF16),
            pltpu.VMEM(fresh, BF16),
            pltpu.VMEM(fresh, BF16),
            pltpu.SemaphoreType.DMA((2 * blocks + 1,)),
            pltpu.SemaphoreType.DMA((blocks * steps,)),
            pltpu.SemaphoreType.DMA((2,)),
        ],
        compiler_params=params(59),
        cost_estimate=cost(1e9, 8 * MIB),
        name="final",
    )(places, *shares, key_weight, value_weight, *small, base_rows, queries, old)


def swap(x, bit):
    count = lax.axis_size("tp")
    return lax.ppermute(x, "tp", [(i, i ^ bit) for i in range(count)])


def per_device(
    normed_input_rows,
    queries,
    key_weight,
    value_weight,
    cached_key_store,
    cached_value_store,
    adapter_down_weight,
    adapter_up_weight,
    adapter_index_rows,
    adapter_rank_list,
    cache_fill_length,
):
    steps, rows_dev, width = normed_input_rows.shape
    total = steps * rows_dev
    replicas = lax.axis_size("rep")
    resident = adapter_down_weight.shape[0]
    columns = key_weight.shape[1]
    groups = columns // HEAD_WIDTH
    heads = queries.shape[2] // columns
    t = lax.axis_index("tp")
    odd = jnp.reshape(t % 2, (1,)).astype(jnp.int32)

    x = normed_input_rows.reshape(total, width)
    cuts = (0, 5 * width // 16, 9 * width // 16, width)
    outgoing, sel = dispatch(adapter_index_rows, x, rows_dev, resident, replicas)
    landed = lax.all_to_all(outgoing, "rep", split_axis=0, concat_axis=0, tiled=True)

    queries, x_near, outgoing = lax.optimization_barrier((queries, x, outgoing))
    q_rows = queries.reshape(steps, rows_dev, groups, heads, HEAD_WIDTH)
    q_rows = q_rows.transpose(1, 2, 0, 3, 4).reshape(rows_dev, groups * steps * heads, HEAD_WIDTH)
    old, lse = stored(cache_fill_length, q_rows, cached_key_store, cached_value_store)

    positions = (
        cache_fill_length[None, :] + jnp.arange(steps, dtype=jnp.int32)[:, None]
    ).reshape(total)
    half = HEAD_WIDTH // 2
    frequency = jnp.power(rope_theta, -(jnp.arange(half, dtype=F32) * (2.0 / HEAD_WIDTH)))
    angles = positions.astype(F32)[:, None] * frequency[None, :]
    cos, sin = jnp.cos(angles), jnp.sin(angles)
    cos = jnp.concatenate([cos, cos], axis=1)
    sin = jnp.concatenate([-sin, sin], axis=1)

    slot = jnp.arange(2 * RANK_PADDED, dtype=jnp.int32) % RANK_PADDED
    factor = jnp.where(
        slot[None, :] < adapter_rank_list[:, None],
        adapter_strength / adapter_rank_list.astype(F32)[:, None],
        0.0,
    )

    near = swap(x_near, 1)
    home = jnp.stack([t, t ^ 1, t ^ 2, t ^ 3]).astype(jnp.int32) * width
    across = home[2:]
    base_rows = base(home[:2], (x, near), key_weight, value_weight)
    landed, old, lse, cos, sin, base_rows, factor = lax.optimization_barrier(
        (landed, old, lse, cos, sin, base_rows, factor)
    )

    part0, _ = lax.optimization_barrier((x_near[:, : cuts[1]], landed))
    far0 = swap(part0, 2)
    keep, send = down(odd, landed, adapter_down_weight, factor)
    part = keep + swap(send, 1)
    part, far0 = lax.optimization_barrier((part, far0))
    arrived = swap(part.astype(BF16), 2)
    part1, _ = lax.optimization_barrier((x_near[:, cuts[1] : cuts[2]], arrived))
    far1 = swap(part1, 2)
    own = (part + arrived.astype(F32)).astype(BF16)
    other = swap(own, 1)
    returned = up(odd, own, other, landed, adapter_up_weight)
    returned, far0, far1, old, part2 = lax.optimization_barrier((returned, far0, far1, old, x_near[:, cuts[2] :]))
    delivered = lax.all_to_all(returned, "rep", split_axis=0, concat_axis=0, tiled=True)

    far2 = swap(part2, 2)
    base_rows = base(
        jnp.concatenate([across, across + cuts[1]]),
        (far0, swap(far0, 1), far1, swap(far1, 1)),
        key_weight, value_weight, base_rows,
    )
    old = old.transpose(1, 0, 2)
    base_rows, old, far2 = lax.optimization_barrier((base_rows, old, far2))
    far2_near = swap(far2, 1)
    base_rows, old, far2_near, delivered = lax.optimization_barrier((base_rows, old, far2_near, delivered))
    out, keys, values = final(
        across + cuts[2], (far2, far2_near), key_weight, value_weight,
        delivered, sel, cos, sin, lse, base_rows, queries, old,
    )
    return out, keys.reshape(steps, rows_dev, columns), values.reshape(steps, rows_dev, columns)


def solution(mesh):
    return jax.shard_map(
        per_device,
        mesh=mesh,
        in_specs=(
            P(None, "rep", "tp"),
            P(None, "rep", "tp"),
            P(None, "tp"),
            P(None, "tp"),
            P("rep", None, "tp"),
            P("rep", None, "tp"),
            P("rep", "tp", None),
            P("rep", None, None, "tp"),
            P(None, "rep"),
            P("rep"),
            P("rep"),
        ),
        out_specs=(P(None, "rep", "tp"), P(None, "rep", "tp"), P(None, "rep", "tp")),
        check_vma=False,
    )
```

```python
import functools
import math

import jax
import jax.numpy as jnp
from jax import lax
from jax.experimental import pallas as pl
from jax.experimental.pallas import tpu as pltpu
from jax.sharding import PartitionSpec as P

HEAD_WIDTH = 128
RANK_PADDED = 128
CAP = 4
LANES = 128

adapter_strength = 16.0
rope_theta = 500000.0
masked_score = -1e30

F32 = jnp.float32
BF16 = jnp.bfloat16
MIB = 1024 * 1024


def cost(flops, moved):
    return pl.CostEstimate(flops=int(flops), bytes_accessed=int(moved), transcendentals=0)


def params(mib, **extra):
    return pltpu.CompilerParams(vmem_limit_bytes=mib * MIB, **extra)


def dispatch_kernel(
    rows_dev, resident, ids_hbm, x_hbm, out_hbm, sel_hbm, ids_ref, x_ref, out_ref, sel_ref, in_sem, out_sem
):
    total = x_ref.shape[0]
    width = x_ref.shape[1]
    slots = out_ref.shape[0]
    per_home = (total // rows_dev) * CAP
    chunk = 512
    places = [slice(start, start + chunk) for start in range(0, width, chunk)]
    count = len(places)
    fetch_ids = pltpu.make_async_copy(ids_hbm, ids_ref, in_sem.at[count])
    fetch_ids.start()
    fetches = [
        pltpu.make_async_copy(x_hbm.at[:, where], x_ref.at[:, where], in_sem.at[i])
        for i, where in enumerate(places)
    ]
    for fetch in fetches:
        fetch.start()
    fetch_ids.wait()
    ids = ids_ref[...]
    sub = lax.broadcasted_iota(jnp.int32, (total, total), 0)
    lane = lax.broadcasted_iota(jnp.int32, (total, total), 1)
    ids_r = jnp.concatenate([ids[s : s + 1] for s in range(total // rows_dev)], axis=1)
    diagonal = jnp.where(sub == lane, ids_r.astype(F32), 0.0)
    ids_c = jnp.sum(diagonal, axis=1, keepdims=True).astype(jnp.int32)
    own_r = lax.div(ids_r, resident)
    own_c = lax.div(ids_c, resident)
    same = (own_c == own_r) & (lax.div(sub, rows_dev) == lax.div(lane, rows_dev))
    before_row = jnp.sum(jnp.where(same & (sub < lane), 1.0, 0.0), axis=0, keepdims=True)
    before_col = jnp.sum(jnp.where(same & (lane < sub), 1.0, 0.0), axis=1, keepdims=True)
    step_r = lax.div(lax.broadcasted_iota(jnp.int32, (1, total), 1), rows_dev)
    step_c = lax.div(lax.broadcasted_iota(jnp.int32, (total, 1), 0), rows_dev)
    place_r = own_r * per_home + step_r * CAP + before_row.astype(jnp.int32)
    place_c = own_c * per_home + step_c * CAP + before_col.astype(jnp.int32)
    sel_ref[...] = jnp.where(
        lax.broadcasted_iota(jnp.int32, (total, slots), 1) == place_c, 1.0, 0.0
    ).astype(BF16)
    spread = jnp.where(
        lax.broadcasted_iota(jnp.int32, (slots, total), 0) == place_r, 1.0, 0.0
    ).astype(BF16)
    local = ids_c - own_c * resident
    marks = jnp.where(
        lax.broadcasted_iota(jnp.int32, (total, LANES), 1) == local, 1.0, 0.0
    ).astype(BF16)
    sends = [pltpu.make_async_copy(sel_ref, sel_hbm, out_sem.at[count])]
    sends[0].start()
    last = slice(width, width + LANES)
    out_ref[:, last] = jnp.dot(spread, marks, preferred_element_type=F32).astype(BF16)
    sends.append(pltpu.make_async_copy(out_ref.at[:, last], out_hbm.at[:, last], out_sem.at[count + 1]))
    sends[1].start()
    for i, where in enumerate(places):
        fetches[i].wait()
        out_ref[:, where] = jnp.dot(spread, x_ref[:, where], preferred_element_type=F32).astype(BF16)
        send = pltpu.make_async_copy(out_ref.at[:, where], out_hbm.at[:, where], out_sem.at[i])
        send.start()
        sends.append(send)
    for send in sends:
        send.wait()


def in_hbm(count):
    return [pl.BlockSpec(memory_space=pltpu.HBM)] * count


def dispatch(ids, x, rows_dev, resident, replicas):
    total, width = x.shape
    slots = replicas * (total // rows_dev) * CAP
    outgoing, sel = (slots, width + LANES), (total, slots)
    return pl.pallas_call(
        functools.partial(dispatch_kernel, rows_dev, resident),
        in_specs=in_hbm(2),
        out_specs=tuple(in_hbm(2)),
        out_shape=(jax.ShapeDtypeStruct(outgoing, BF16), jax.ShapeDtypeStruct(sel, BF16)),
        scratch_shapes=[
            pltpu.VMEM(ids.shape, jnp.int32),
            pltpu.VMEM(x.shape, BF16),
            pltpu.VMEM(outgoing, BF16),
            pltpu.VMEM(sel, BF16),
            pltpu.SemaphoreType.DMA((width // 512 + 1,)),
            pltpu.SemaphoreType.DMA((width // 512 + 2,)),
        ],
        compiler_params=params(60),
        cost_estimate=cost(2 * slots * total * width, 2 * (total + slots) * width),
        name="dispatch",
    )(ids, x)


def mark_column(tail, index):
    lane = lax.broadcasted_iota(jnp.int32, tail.shape, 1)
    return jnp.sum(jnp.where(lane == index, tail.astype(F32), 0.0), axis=1, keepdims=True)


def down_kernel(odd_ref, landed_ref, weight_ref, factor_ref, keep_ref, send_ref, sum_ref):
    a = pl.program_id(0)
    width = weight_ref.shape[1]
    half = keep_ref.shape[0]
    product = jnp.dot(landed_ref[:, :width], weight_ref[0], preferred_element_type=F32)
    part = product * (mark_column(landed_ref[:, width:], a) * factor_ref[0])

    @pl.when(a == 0)
    def _():
        sum_ref[...] = part

    @pl.when(a > 0)
    def _():
        sum_ref[...] += part

    @pl.when(a == pl.num_programs(0) - 1)
    def _():
        odd = odd_ref[0] == 1
        low, high = sum_ref[:half], sum_ref[half:]
        keep_ref[...] = jnp.where(odd, high, low)
        send_ref[...] = jnp.where(odd, low, high)


def down(odd, landed, weight, factor):
    slots, wide = landed.shape
    count, width, ranks = weight.shape
    half = jax.ShapeDtypeStruct((slots // 2, ranks), F32)
    kept = pl.BlockSpec((slots // 2, ranks), lambda a, p: (0, 0))
    return pl.pallas_call(
        down_kernel,
        grid_spec=pltpu.PrefetchScalarGridSpec(
            num_scalar_prefetch=1,
            grid=(count,),
            in_specs=[
                pl.BlockSpec((slots, wide), lambda a, p: (0, 0)),
                pl.BlockSpec((1, width, ranks), lambda a, p: (a, 0, 0)),
                pl.BlockSpec((1, 1, ranks), lambda a, p: (a, 0, 0)),
            ],
            out_specs=(kept, kept),
            scratch_shapes=[pltpu.VMEM((slots, ranks), F32)],
        ),
        out_shape=(half, half),
        compiler_params=params(16),
        cost_estimate=cost(2 * count * slots * width * ranks, 2 * (slots * wide + count * width * ranks)),
        name="down",
    )(odd, landed, weight, factor.reshape(count, 1, ranks))


def up_kernel(odd_ref, own_ref, other_ref, tail_ref, weight_ref, out_ref):
    count, _, ranks, columns = weight_ref.shape
    odd = odd_ref[0] == 1
    tail = tail_ref[...]
    marks = [mark_column(tail, a).astype(BF16) for a in range(count)]
    own, other = own_ref[...].astype(F32), other_ref[...].astype(F32)
    whole = jnp.concatenate([jnp.where(odd, other, own), jnp.where(odd, own, other)], axis=0).astype(BF16)
    for u in range(2):
        mid = whole[:, u * ranks : (u + 1) * ranks]
        total = None
        for a in range(count):
            term = jnp.dot(mid * marks[a], weight_ref[a, u], preferred_element_type=F32)
            total = term if total is None else total + term
        out_ref[:, u * columns : (u + 1) * columns] = total.astype(BF16)


def up(odd, own, other, landed, weight):
    slots = landed.shape[0]
    count, _, ranks, columns = weight.shape
    last = landed.shape[1] // LANES - 1
    half = pl.BlockSpec(own.shape, lambda i, p: (0, 0))
    return pl.pallas_call(
        up_kernel,
        grid_spec=pltpu.PrefetchScalarGridSpec(
            num_scalar_prefetch=1,
            grid=(1,),
            in_specs=[
                half,
                half,
                pl.BlockSpec((slots, LANES), lambda i, p: (0, last)),
                pl.BlockSpec(weight.shape, lambda i, p: (0, 0, 0, 0)),
            ],
            out_specs=pl.BlockSpec((slots, 2 * columns), lambda i, p: (0, 0)),
        ),
        out_shape=jax.ShapeDtypeStruct((slots, 2 * columns), BF16),
        compiler_params=params(16),
        cost_estimate=cost(4 * count * slots * ranks * columns, 4 * slots * columns),
        name="up",
    )(odd, own, other, landed, weight)


def share_copies(place_ref, shares, key_hbm, value_hbm, share_refs, weight_refs, sem):
    copies = []
    for i, (share, x_ref, w_ref) in enumerate(zip(shares, share_refs, weight_refs)):
        unit = x_ref.shape[1]
        rows = pl.ds(pl.multiple_of(place_ref[i], LANES), unit)
        copies.append(
            [
                pltpu.make_async_copy(share, x_ref, sem.at[i, 0]),
                pltpu.make_async_copy(key_hbm.at[rows, :], w_ref.at[0], sem.at[i, 1]),
                pltpu.make_async_copy(value_hbm.at[rows, :], w_ref.at[1], sem.at[i, 2]),
            ]
        )
    return copies


def share_scratch(shares, columns):
    return (
        [pltpu.VMEM(x.shape, BF16) for x in shares]
        + [pltpu.VMEM((2, x.shape[1], columns), BF16) for x in shares]
        + [pltpu.SemaphoreType.DMA((max(1, len(shares)), 3))]
    )


def base_kernel(count, more, place_ref, *refs):
    shares, refs = refs[:count], refs[count:]
    key_hbm, value_hbm = refs[:2]
    before = refs[2] if more else None
    refs = refs[3:] if more else refs[2:]
    out_hbm, refs = refs[0], refs[1:]
    share_refs, weight_refs, sem = refs[:count], refs[count : 2 * count], refs[2 * count]
    out_ref, out_sem = refs[2 * count + 1 :]
    copies = share_copies(place_ref, shares, key_hbm, value_hbm, share_refs, weight_refs, sem)
    for group in copies:
        for copy in group:
            copy.start()
    if more:
        load = pltpu.make_async_copy(before, out_ref, out_sem.at[2])
        load.start()
    columns = key_hbm.shape[1]
    totals = [None, None]
    for i in range(count):
        copies[i][0].wait()
        for number in range(2):
            copies[i][1 + number].wait()
            term = jnp.dot(share_refs[i][...], weight_refs[i][number], preferred_element_type=F32)
            totals[number] = term if i == 0 else totals[number] + term
    if more:
        load.wait()
    stores = []
    for number in range(2):
        where = slice(number * columns, (number + 1) * columns)
        out_ref[:, where] = totals[number] + out_ref[:, where] if more else totals[number]
        store = pltpu.make_async_copy(out_ref.at[:, where], out_hbm.at[:, where], out_sem.at[number])
        store.start()
        stores.append(store)
    for store in stores:
        store.wait()


def base(places, shares, key_weight, value_weight, before=None):
    total = shares[0].shape[0]
    count = len(shares)
    columns = key_weight.shape[1]
    more = () if before is None else (before,)
    return pl.pallas_call(
        functools.partial(base_kernel, count, before is not None),
        in_specs=[pl.BlockSpec(memory_space=pltpu.SMEM)] + in_hbm(count + 2 + len(more)),
        out_specs=in_hbm(1)[0],
        out_shape=jax.ShapeDtypeStruct((total, 2 * columns), F32),
        scratch_shapes=share_scratch(shares, columns)
        + [pltpu.VMEM((total, 2 * columns), F32), pltpu.SemaphoreType.DMA((3,))],
        compiler_params=params(60),
        cost_estimate=cost(0, 0),
        name="base",
    )(places, *shares, key_weight, value_weight, *more)


def stored_kernel(rows, length_ref, q_ref, k_ref, v_ref, out_ref, lse_ref):
    first = pl.program_id(0) * rows
    slots = k_ref.shape[1]
    groups = k_ref.shape[2] // HEAD_WIDTH
    per_group = q_ref.shape[1] // groups
    scale = 1.0 / math.sqrt(HEAD_WIDTH)
    lane = lax.broadcasted_iota(jnp.int32, (per_group, slots), 1)
    pieces = [
        (r, slice(g * per_group, (g + 1) * per_group), slice(g * HEAD_WIDTH, (g + 1) * HEAD_WIDTH))
        for r in range(rows)
        for g in range(groups)
    ]
    raw = [
        lax.dot_general(
            q_ref[r, mine, :], k_ref[r, :, head], (((1,), (1,)), ((), ())), preferred_element_type=F32
        )
        for r, mine, head in pieces
    ]
    shares = []
    for (r, mine, head), scores in zip(pieces, raw):
        scores = jnp.where(lane < length_ref[first + r], scores * scale, masked_score)
        top = jnp.max(scores, axis=1, keepdims=True)
        weights = jnp.exp(scores - top)
        shares.append((weights.astype(BF16), top, jnp.sum(weights, axis=1, keepdims=True)))
    mixed = [
        jnp.dot(weights, v_ref[r, :, head], preferred_element_type=F32)
        for (r, mine, head), (weights, top, norm) in zip(pieces, shares)
    ]
    @pl.when(first == 0)
    def _():
        lse_ref[...] = jnp.zeros_like(lse_ref)

    logs = [[] for _ in range(rows)]
    for (r, mine, head), (weights, top, norm), value in zip(pieces, shares, mixed):
        out_ref[r, mine, :] = value / norm
        logs[r].append(top + jnp.log(norm))
    table = lse_ref[...]
    at = lax.broadcasted_iota(jnp.int32, table.shape, 1)
    for r in range(rows):
        table = jnp.where(at == first + r, jnp.concatenate(logs[r], axis=0), table)
    lse_ref[...] = table


def stored(lengths, q_rows, keys, values):
    count, slots, width = keys.shape
    rows = 8
    queries = q_rows.shape[1]
    block = pl.BlockSpec((rows, queries, HEAD_WIDTH), lambda i, n: (i, 0, 0))
    cache = pl.BlockSpec((rows, slots, width), lambda i, n: (i, 0, 0))
    return pl.pallas_call(
        functools.partial(stored_kernel, rows),
        grid_spec=pltpu.PrefetchScalarGridSpec(
            num_scalar_prefetch=1,
            grid=(count // rows,),
            in_specs=[block, cache, cache],
            out_specs=(block, pl.BlockSpec((queries, count), lambda i, n: (0, 0))),
        ),
        out_shape=(
            jax.ShapeDtypeStruct((count, queries, HEAD_WIDTH), F32),
            jax.ShapeDtypeStruct((queries, count), F32),
        ),
        compiler_params=params(60),
        cost_estimate=cost(4 * count * queries * slots * HEAD_WIDTH, 4 * count * slots * width),
        name="stored",
    )(lengths, q_rows, keys, values)


def final_kernel(steps, count, place_ref, *refs):
    shares, refs = refs[:count], refs[count:]
    key_weight, value_weight, refs = refs[0], refs[1], refs[2:]
    small, base_hbm, q_hbm, old_hbm, out_hbm, key_hbm, value_hbm = refs[:5], *refs[5:11]
    refs = refs[11:]
    share_refs, weight_refs, share_sem = refs[:count], refs[count : 2 * count], refs[2 * count]
    refs = refs[2 * count + 1 :]
    small_refs, small_sem, refs = refs[:5], refs[5], refs[6:]
    base_ref, q_ref, old_ref, out_ref, key_ref, value_ref, in_sem, out_sem, new_sem = refs
    delivered_ref, sel_ref, cos_ref, sin_ref, lse_ref = small_refs
    total, wide = base_ref.shape
    rows_dev = total // steps
    columns = wide // 2
    groups = columns // HEAD_WIDTH
    heads = q_ref.shape[2] // columns
    block = min(rows_dev, LANES // steps)
    here = steps * block
    blocks = [slice(start, start + block) for start in range(0, rows_dev, block)]
    scale = 1.0 / math.sqrt(HEAD_WIDTH)
    early = [pltpu.make_async_copy(a, b, small_sem.at[i]) for i, (a, b) in enumerate(zip(small, small_refs))]
    fetch_base = pltpu.make_async_copy(base_hbm, base_ref, in_sem.at[2 * len(blocks)])
    copies = share_copies(place_ref, shares, key_weight, value_weight, share_refs, weight_refs, share_sem)
    for copy in early[:2] + [fetch_base] + sum(copies, []) + early[2:]:
        copy.start()
    fetches = []
    for b, rows in enumerate(blocks):
        fetches.append(
            (
                pltpu.make_async_copy(q_hbm.at[:, rows, :], q_ref.at[:, rows, :], in_sem.at[2 * b]),
                pltpu.make_async_copy(old_hbm.at[:, rows, :], old_ref.at[:, rows, :], in_sem.at[2 * b + 1]),
            )
        )
        for fetch in fetches[-1]:
            fetch.start()

    for copy in early[:2]:
        copy.wait()
    delta = jnp.dot(sel_ref[...], delivered_ref[...], preferred_element_type=F32)
    fetch_base.wait()
    summed = base_ref[...] + delta
    halves = [summed[:, :columns], summed[:, columns:]]
    for i in range(count):
        copies[i][0].wait()
        for number in range(2):
            copies[i][1 + number].wait()
            halves[number] += jnp.dot(share_refs[i][...], weight_refs[i][number], preferred_element_type=F32)
    for copy in early[2:]:
        copy.wait()
    ones = jnp.ones((total, LANES), BF16)
    keys, both = [], []
    for g in range(groups):
        head = slice(g * HEAD_WIDTH, (g + 1) * HEAD_WIDTH)
        piece = halves[0][:, head]
        turned = piece * cos_ref[...] + pltpu.roll(piece, HEAD_WIDTH // 2, 1) * sin_ref[...]
        keys.append(turned.astype(BF16))
        key_ref[:, head] = keys[-1]
        fresh = halves[1][:, head].astype(BF16)
        value_ref[:, head] = fresh
        both.append(jnp.concatenate([fresh, ones], axis=1))
    sends = [
        pltpu.make_async_copy(key_ref, key_hbm, new_sem.at[0]),
        pltpu.make_async_copy(value_ref, value_hbm, new_sem.at[1]),
    ]
    for send in sends:
        send.start()

    sub = lax.broadcasted_iota(jnp.int32, (heads * block, here), 0)
    lane = lax.broadcasted_iota(jnp.int32, (heads * block, here), 1)
    same_row = lax.rem(sub, block) == lax.rem(lane, block)
    of_step = lax.div(lane, block)
    first_key = same_row & (of_step == 0)
    all_ones = jnp.ones((here, LANES), BF16)
    pieces = [(g, t) for t in range(steps) for g in range(groups)]

    def lanes(g, h):
        return slice((g * heads + h) * HEAD_WIDTH, (g * heads + h + 1) * HEAD_WIDTH)

    def of_block(array, rows):
        return jnp.concatenate(
            [array[s * rows_dev + rows.start : s * rows_dev + rows.stop] for s in range(steps)], axis=0
        )

    for b, rows in enumerate(blocks):
        own_keys = [of_block(k, rows) for k in keys]
        own_both = [of_block(v, rows) for v in both]
        logs = lse_ref[:, rows]
        logs = jnp.concatenate([logs] * steps, axis=1)
        fetches[b][0].wait()
        raw = []
        for g, t in pieces:
            q = jnp.concatenate([q_ref[t, rows, lanes(g, h)] for h in range(heads)], axis=0)
            raw.append(lax.dot_general(q, own_keys[g], (((1,), (1,)), ((), ())), preferred_element_type=F32))
        shares = []
        for (g, t), scores in zip(pieces, raw):
            first = (g * steps + t) * heads
            lse = jnp.concatenate(
                [jnp.broadcast_to(logs[first + h : first + h + 1], (block, here)) for h in range(heads)], axis=0
            )
            lse = jnp.where(first_key, lse, masked_score)
            scores = jnp.where(same_row & (of_step <= t), scores * scale, masked_score)
            top = jnp.max(jnp.maximum(lse, scores), axis=1, keepdims=True)
            shares.append((jnp.exp(scores - top).astype(BF16), jnp.exp(lse - top).astype(BF16)))
        mixed = [
            (
                jnp.dot(w, own_both[g], preferred_element_type=F32),
                jnp.dot(kept, all_ones, preferred_element_type=F32),
            )
            for (g, t), (w, kept) in zip(pieces, shares)
        ]
        fetches[b][1].wait()
        for (g, t), (value, kept) in zip(pieces, mixed):
            first = (g * steps + t) * heads
            old = old_ref[first : first + heads, rows, :].reshape(heads * block, HEAD_WIDTH)
            result = (old * kept + value[:, :HEAD_WIDTH]) / (kept + value[:, HEAD_WIDTH:])
            result = result.astype(BF16)
            for h in range(heads):
                out_ref[t, rows, lanes(g, h)] = result[h * block : (h + 1) * block]
            if g == groups - 1:
                send = pltpu.make_async_copy(
                    out_ref.at[t, rows, :], out_hbm.at[t, rows, :], out_sem.at[b * steps + t]
                )
                send.start()
                sends.append(send)
    for send in sends:
        send.wait()


def final(places, shares, key_weight, value_weight, delivered, sel, cos, sin, lse, base_rows, queries, old):
    steps, rows_dev, width = queries.shape
    total, wide = base_rows.shape
    blocks = rows_dev // min(rows_dev, LANES // steps)
    fresh = (total, wide // 2)
    count = len(shares)
    small = (delivered, sel, cos, sin, lse)
    return pl.pallas_call(
        functools.partial(final_kernel, steps, count),
        in_specs=[pl.BlockSpec(memory_space=pltpu.SMEM)] + in_hbm(count + 10),
        out_specs=tuple(in_hbm(3)),
        out_shape=(
            jax.ShapeDtypeStruct(queries.shape, BF16),
            jax.ShapeDtypeStruct(fresh, BF16),
            jax.ShapeDtypeStruct(fresh, BF16),
        ),
        scratch_shapes=share_scratch(shares, wide // 2)
        + [pltpu.VMEM(array.shape, array.dtype) for array in small]
        + [
            pltpu.SemaphoreType.DMA((len(small),)),
            pltpu.VMEM(base_rows.shape, F32),
            pltpu.VMEM(queries.shape, BF16),
            pltpu.VMEM(old.shape, F32),
            pltpu.VMEM(queries.shape, BF16),
            pltpu.VMEM(fresh, BF16),
            pltpu.VMEM(fresh, BF16),
            pltpu.SemaphoreType.DMA((2 * blocks + 1,)),
            pltpu.SemaphoreType.DMA((blocks * steps,)),
            pltpu.SemaphoreType.DMA((2,)),
        ],
        compiler_params=params(59),
        cost_estimate=cost(1e9, 8 * MIB),
        name="final",
    )(places, *shares, key_weight, value_weight, *small, base_rows, queries, old)


def swap(x, bit):
    count = lax.axis_size("tp")
    return lax.ppermute(x, "tp", [(i, i ^ bit) for i in range(count)])


def per_device(
    normed_input_rows,
    queries,
    key_weight,
    value_weight,
    cached_key_store,
    cached_value_store,
    adapter_down_weight,
    adapter_up_weight,
    adapter_index_rows,
    adapter_rank_list,
    cache_fill_length,
):
    steps, rows_dev, width = normed_input_rows.shape
    total = steps * rows_dev
    replicas = lax.axis_size("rep")
    resident = adapter_down_weight.shape[0]
    columns = key_weight.shape[1]
    groups = columns // HEAD_WIDTH
    heads = queries.shape[2] // columns
    t = lax.axis_index("tp")
    odd = jnp.reshape(t % 2, (1,)).astype(jnp.int32)

    x = normed_input_rows.reshape(total, width)
    cuts = (0, 5 * width // 16, 8 * width // 16, width)
    outgoing, sel = dispatch(adapter_index_rows, x, rows_dev, resident, replicas)
    landed = lax.all_to_all(outgoing, "rep", split_axis=0, concat_axis=0, tiled=True)

    queries, x_near, outgoing = lax.optimization_barrier((queries, x, outgoing))
    q_rows = queries.reshape(steps, rows_dev, groups, heads, HEAD_WIDTH)
    q_rows = q_rows.transpose(1, 2, 0, 3, 4).reshape(rows_dev, groups * steps * heads, HEAD_WIDTH)
    old, lse = stored(cache_fill_length, q_rows, cached_key_store, cached_value_store)

    positions = (
        cache_fill_length[None, :] + jnp.arange(steps, dtype=jnp.int32)[:, None]
    ).reshape(total)
    half = HEAD_WIDTH // 2
    frequency = jnp.power(rope_theta, -(jnp.arange(half, dtype=F32) * (2.0 / HEAD_WIDTH)))
    angles = positions.astype(F32)[:, None] * frequency[None, :]
    cos, sin = jnp.cos(angles), jnp.sin(angles)
    cos = jnp.concatenate([cos, cos], axis=1)
    sin = jnp.concatenate([-sin, sin], axis=1)

    slot = jnp.arange(2 * RANK_PADDED, dtype=jnp.int32) % RANK_PADDED
    factor = jnp.where(
        slot[None, :] < adapter_rank_list[:, None],
        adapter_strength / adapter_rank_list.astype(F32)[:, None],
        0.0,
    )

    near = swap(x_near, 1)
    home = jnp.stack([t, t ^ 1, t ^ 2, t ^ 3]).astype(jnp.int32) * width
    across = home[2:]
    base_rows = base(home[:2], (x, near), key_weight, value_weight)
    landed, old, lse, cos, sin, base_rows, factor = lax.optimization_barrier(
        (landed, old, lse, cos, sin, base_rows, factor)
    )

    part0, _ = lax.optimization_barrier((x_near[:, : cuts[1]], landed))
    far0 = swap(part0, 2)
    keep, send = down(odd, landed, adapter_down_weight, factor)
    part = keep + swap(send, 1)
    part, far0 = lax.optimization_barrier((part, far0))
    arrived = swap(part.astype(BF16), 2)
    part1, _ = lax.optimization_barrier((x_near[:, cuts[1] : cuts[2]], arrived))
    far1 = swap(part1, 2)
    own = (part + arrived.astype(F32)).astype(BF16)
    other = swap(own, 1)
    returned = up(odd, own, other, landed, adapter_up_weight)
    returned, far0, far1, old, part2 = lax.optimization_barrier((returned, far0, far1, old, x_near[:, cuts[2] :]))
    delivered = lax.all_to_all(returned, "rep", split_axis=0, concat_axis=0, tiled=True)

    far2 = swap(part2, 2)
    base_rows = base(
        jnp.concatenate([across, across + cuts[1]]),
        (far0, swap(far0, 1), far1, swap(far1, 1)),
        key_weight, value_weight, base_rows,
    )
    old = old.transpose(1, 0, 2)
    base_rows, old, far2 = lax.optimization_barrier((base_rows, old, far2))
    far2_near = swap(far2, 1)
    base_rows, old, far2_near, delivered = lax.optimization_barrier((base_rows, old, far2_near, delivered))
    out, keys, values = final(
        across + cuts[2], (far2, far2_near), key_weight, value_weight,
        delivered, sel, cos, sin, lse, base_rows, queries, old,
    )
    return out, keys.reshape(steps, rows_dev, columns), values.reshape(steps, rows_dev, columns)


def solution(mesh):
    return jax.shard_map(
        per_device,
        mesh=mesh,
        in_specs=(
            P(None, "rep", "tp"),
            P(None, "rep", "tp"),
            P(None, "tp"),
            P(None, "tp"),
            P("rep", None, "tp"),
            P("rep", None, "tp"),
            P("rep", "tp", None),
            P("rep", None, None, "tp"),
            P(None, "rep"),
            P("rep"),
            P("rep"),
        ),
        out_specs=(P(None, "rep", "tp"), P(None, "rep", "tp"), P(None, "rep", "tp")),
        check_vma=False,
    )
```
